32 devices in a mesh: dp: 8 (over y, x, core), ctx: 4 (over z).
Axes of the slice: x: 2, y: 2, z: 4, core: 2. Of those that a mesh axis runs over, the one named last changes fastest.
Arguments:
- queries: bfloat16 [4096, 512], P(('dp', 'ctx')), may hold values from -25 to 25
- keys: bfloat16 [4096, 128], P(('dp', 'ctx')), may hold values from -6 to 6
- values: bfloat16 [4096, 128], P(('dp', 'ctx')), may hold values from -6 to 6
- out_grad: bfloat16 [4096, 512], P(('dp', 'ctx')), may hold values from -7 to 7
- doc_lengths: int32 [8, 17], P('dp'), may hold values from 0 to 512, as said below
- source_slot: int32 [4096], P(('dp', 'ctx')), may hold values from 0 to 127, as said below
Outputs:
- attended: bfloat16 [4096, 512], P(('dp', 'ctx'))
- query_grad: bfloat16 [4096, 512], P(('dp', 'ctx'))
- key_grad: bfloat16 [4096, 128], P(('dp', 'ctx'))
- value_grad: bfloat16 [4096, 128], P(('dp', 'ctx'))
The draws below stay inside these ranges and needn't reach their ends.
Inputs may be any that keep to these rules, and one draw needn't show every extreme that they name: `doc_lengths`: row d lists group d's documents in order: the first covers devices 0 to m - 1 of the group whole (m * 128 tokens, 1 <= m <= 4, with m = 4 in row 0), then 4 documents of positive length for each later device that fill that device exactly, then zeros; every row sums to 512. `source_slot`: on each device the 128 entries are a permutation of 0 to 127.
All inputs are finite; a program needn't handle non-finite values.
Results may differ from the reference program's by a relative error of at most 0.033.
Values may be sent and summed in bfloat16 or wider, within the bound.
No kernel may reach another device: no remote copies, remote signals or barrier semaphores. Data moves between devices by JAX's collectives and lax.ppermute only.
A program may use at most 64 MiB of HBM per device.

```python
import jax
import jax.numpy as jnp
from jax import lax

DH = 128
HQ = 4
TOK_DEV = 128
SHORT_DEV = 4
GROUP = 512
TOKENS = 4096
N_DP = 8
N_CTX = 4


def plan_slots(key):
    devices = TOKENS // TOK_DEV
    raw_scores = jax.random.randint(jax.random.fold_in(key, 11), (devices, TOK_DEV), 0, 2 ** 20, dtype=jnp.int32)
    raw_scores = raw_scores * TOK_DEV + jnp.arange(TOK_DEV, dtype=jnp.int32)[None, :]
    return jnp.argsort(raw_scores, axis=1).astype(jnp.int32).reshape(TOKENS)


def arrival_index_drawn(slots):
    ctx_count = GROUP // TOK_DEV
    peer_rows = TOK_DEV // (TOKENS // GROUP)
    global_row = jnp.arange(TOKENS, dtype=jnp.int32)
    device = global_row // TOK_DEV
    group_index = device // ctx_count
    ctx_index = device % ctx_count
    return (slots // peer_rows * ctx_count + ctx_index) * TOK_DEV + group_index * peer_rows + slots % peer_rows


def doc_table(key):
    group_count = TOKENS // GROUP
    ctx_count = GROUP // TOK_DEV
    span_devices = jax.random.randint(jax.random.fold_in(key, 21), (group_count,), 1, ctx_count + 1, dtype=jnp.int32)
    span_devices = span_devices.at[0].set(ctx_count)
    candidates = TOK_DEV - 1
    raw_scores = jax.random.randint(jax.random.fold_in(key, 22), (group_count, ctx_count, candidates), 0, 2 ** 20, dtype=jnp.int32)
    raw_scores = raw_scores * candidates + jnp.arange(candidates, dtype=jnp.int32)[None, None, :]
    cut_points = jnp.sort(jnp.argsort(raw_scores, axis=2)[:, :, :SHORT_DEV - 1].astype(jnp.int32) + 1, axis=2)
    bounds = jnp.concatenate([jnp.zeros((group_count, ctx_count, 1), jnp.int32), cut_points, jnp.full((group_count, ctx_count, 1), TOK_DEV, jnp.int32)], axis=2)
    short_lengths = (bounds[:, :, 1:] - bounds[:, :, :-1]).reshape(group_count, ctx_count * SHORT_DEV)
    shifted = jnp.arange(ctx_count * SHORT_DEV, dtype=jnp.int32)[None, :] + span_devices[:, None] * SHORT_DEV
    taken_lengths = jnp.take_along_axis(short_lengths, jnp.minimum(shifted, ctx_count * SHORT_DEV - 1), axis=1)
    taken_lengths = jnp.where(shifted < ctx_count * SHORT_DEV, taken_lengths, 0)
    return jnp.concatenate([span_devices[:, None] * TOK_DEV, taken_lengths], axis=1).astype(jnp.int32)


def drawn_rows(key):
    key_rows = jax.random.truncated_normal(jax.random.fold_in(key, 31), -6.0, 6.0, (TOKENS, DH), jnp.float32)
    query_rows = jax.random.truncated_normal(jax.random.fold_in(key, 32), -6.0, 6.0, (TOKENS, HQ * DH), jnp.float32)
    return (query_rows, key_rows)


def draw_queries(key, part):
    query_rows, key_rows = drawn_rows(key)
    target = arrival_index_drawn(plan_slots(key))
    return jnp.zeros((TOKENS, HQ * DH), jnp.float32).at[target].set(query_rows).astype(jnp.bfloat16)


def draw_keys(key, part):
    query_rows, key_rows = drawn_rows(key)
    target = arrival_index_drawn(plan_slots(key))
    return jnp.zeros((TOKENS, DH), jnp.float32).at[target].set(key_rows).astype(jnp.bfloat16)


def draw_out_grad(key, part):
    ctx_count = GROUP // TOK_DEV
    noise = jax.random.truncated_normal(jax.random.fold_in(key, 41), -6.0, 6.0, (TOKENS, HQ * DH), jnp.float32)
    column_signs = (2 * jax.random.randint(jax.random.fold_in(key, 42), (HQ * DH,), 0, 2, dtype=jnp.int32) - 1).astype(jnp.float32)
    global_row = jnp.arange(TOKENS, dtype=jnp.int32)
    ctx_index = global_row // TOK_DEV % ctx_count
    later = (2 * ctx_index >= ctx_count).astype(jnp.float32)
    grad_rows = noise + later[:, None] * column_signs[None, :]
    target = arrival_index_drawn(plan_slots(key))
    return jnp.zeros((TOKENS, HQ * DH), jnp.float32).at[target].set(grad_rows).astype(jnp.bfloat16)


def draw_doc_lengths(key, part):
    return doc_table(key)


def draw_source_slot(key, part):
    return plan_slots(key)


def levels(rng, shape, cuts, smallest, top_value):
    def one(axis_at, shards_of):
        steps = jax.random.uniform(jax.random.fold_in(jax.random.fold_in(rng, 6), axis_at), (shards_of,), jnp.float32, smallest / len(cuts), top_value / len(cuts))
        return jnp.repeat(jnp.exp(steps), shape[axis_at] // shards_of).reshape((-1,) + (1,) * (len(shape) - axis_at - 1))

    gain = one(*cuts[0])
    for cut in cuts[1:]:
        gain = gain * one(*cut)
    return gain


def normal_values(key, dims, scale, limit, pieces=(), held_as=jnp.bfloat16):
    entries = scale * jax.random.normal(key, dims, jnp.float32)
    if pieces:
        entries = entries * levels(key, dims, pieces, -0.22, 0.18)
    return jnp.clip(entries, -limit, limit).astype(held_as)


def setup_inputs(seed: int = 0) -> dict:
    seeds = jax.random.split(jax.random.key(seed), 7)
    queries = draw_queries(jax.random.fold_in(seeds[6], 71), 0)
    keys = draw_keys(jax.random.fold_in(seeds[6], 71), 0)
    values = normal_values(seeds[2], (TOKENS, DH), 1.0, 6.0, ((0, 32),))
    out_grad = draw_out_grad(jax.random.fold_in(seeds[6], 71), 0)
    doc_lengths = draw_doc_lengths(jax.random.fold_in(seeds[6], 71), 0)
    source_slot = draw_source_slot(jax.random.fold_in(seeds[6], 71), 0)
    return dict(queries=queries, keys=keys, values=values, out_grad=out_grad, doc_lengths=doc_lengths, source_slot=source_slot)


def arrival_index(source_slot):
    peer_rows = TOK_DEV // N_DP
    global_row = jnp.arange(TOKENS, dtype=jnp.int32)
    device = global_row // TOK_DEV
    group_index = device // N_CTX
    ctx_index = device % N_CTX
    return ((source_slot // peer_rows) * N_CTX + ctx_index) * TOK_DEV + group_index * peer_rows + source_slot % peer_rows


def narrowed(values_in):
    rounded = values_in.astype(jnp.bfloat16)
    return lax.optimization_barrier(rounded).astype(jnp.float32)


def one_group(group_data):
    query_rows, key_rows, value_rows, grad_rows, lengths = group_data
    score_scale = DH ** -0.5
    position = jnp.arange(GROUP, dtype=jnp.int32)
    doc_ends = jnp.cumsum(lengths, dtype=jnp.int32)
    doc = jnp.sum((position[:, None] >= doc_ends[None, :]).astype(jnp.int32), axis=1, dtype=jnp.int32)
    seen = (doc[:, None] == doc[None, :]) & (position[None, :] <= position[:, None])
    query_f = query_rows.astype(jnp.float32)
    key_f = key_rows.astype(jnp.float32)
    value_f = value_rows.astype(jnp.float32)
    grad_f = grad_rows.astype(jnp.float32)
    scores = jnp.einsum("thd,sd->hts", query_f, key_f) * score_scale
    log_total = jax.nn.logsumexp(jnp.where(seen[None], scores, -jnp.inf), axis=2)
    probs = jnp.where(seen[None], jnp.exp(scores - log_total[:, :, None]), 0.0)
    probs_low = narrowed(probs)
    attended = jnp.einsum("hts,sd->thd", probs_low, value_f).astype(jnp.bfloat16)
    row_delta = jnp.sum(grad_f * attended.astype(jnp.float32), axis=2)
    prob_grad = jnp.einsum("thd,sd->hts", grad_f, value_f)
    score_grad = narrowed(probs * (prob_grad - row_delta.T[:, :, None]))
    query_grad = (jnp.einsum("hts,sd->thd", score_grad, key_f) * score_scale).astype(jnp.bfloat16)
    key_grad = (jnp.einsum("hts,thd->sd", score_grad, query_f) * score_scale).astype(jnp.bfloat16)
    value_grad = jnp.einsum("hts,thd->sd", probs_low, grad_f).astype(jnp.bfloat16)
    return attended, query_grad, key_grad, value_grad


def reference(queries, keys, values, out_grad, doc_lengths, source_slot):
    target = arrival_index(source_slot)
    query_rows = queries[target].reshape(N_DP, GROUP, HQ, DH)
    key_rows = keys[target].reshape(N_DP, GROUP, DH)
    value_rows = values[target].reshape(N_DP, GROUP, DH)
    grad_rows = out_grad[target].reshape(N_DP, GROUP, HQ, DH)
    attended, query_grad, key_grad, value_grad = lax.map(one_group, (query_rows, key_rows, value_rows, grad_rows, doc_lengths))

    def placed(computed, template):
        return jnp.zeros_like(template).at[target].set(computed.reshape(template.shape))

    return (placed(attended, queries), placed(query_grad, queries), placed(key_grad, keys), placed(value_grad, values))
```

```python
import functools

import jax
import jax.numpy as jnp
from jax import lax
from jax.experimental import pallas as pl
from jax.experimental.pallas import tpu as pltpu
from jax.sharding import PartitionSpec as P

HIDDEN = -1e30
VMEM = pl.BlockSpec(memory_space=pltpu.VMEM)
SMEM = pl.BlockSpec(memory_space=pltpu.SMEM)


def contract(left, right):
    return lax.dot_general(
        left, right, (((1,), (1,)), ((), ())), preferred_element_type=jnp.float32
    )


def multiply(left, right):
    return jnp.dot(left, right, preferred_element_type=jnp.float32)


def params(mib):
    return pltpu.CompilerParams(vmem_limit_bytes=mib * 1024 * 1024)


def slots_of(rows, peer, own, swapped):
    row = lax.broadcasted_iota(jnp.int32, (rows, rows), 1)
    if not swapped:
        return row
    return lax.bitwise_xor(row // peer, own) * peer + row % peer


def mask_kernel(peer, swapped, place, lengths, slot_row, bias):
    rows = slot_row.shape[1]
    own, first = place[0], place[1] * rows
    slot = jnp.broadcast_to(slot_row[...], (rows, rows))
    along = lax.broadcasted_iota(jnp.int32, (rows, rows), 1)
    down = lax.broadcasted_iota(jnp.int32, (rows, rows), 0)
    key_pos = jnp.sum(jnp.where(slot == down, along, 0), axis=1, keepdims=True)
    slot_down = slot.astype(jnp.float32).T.astype(jnp.int32)
    wanted = slots_of(rows, peer, own, swapped)
    query_pos = jnp.sum(jnp.where(slot_down == wanted, down, 0), axis=0, keepdims=True)

    def later(k, carry):
        end, start = carry
        end = end + lengths[0, k]
        return end, jnp.where(query_pos + first >= end, end, start)

    _, doc_start = lax.fori_loop(
        0, lengths.shape[1], later, (jnp.int32(0), jnp.zeros((1, rows), jnp.int32))
    )
    seen = (key_pos <= query_pos) & (key_pos + first >= doc_start)
    bias[...] = jnp.where(seen, 0.0, HIDDEN)


def pack_kernel(peer, place, queries, out_grad, *pieces):
    own = place[0]
    width = queries.shape[1]
    for index, piece in enumerate(pieces):
        start = pl.multiple_of(lax.bitwise_xor(own, index) * peer, peer)
        piece[:, :width] = queries[pl.ds(start, peer), :]
        piece[:, width:] = out_grad[pl.ds(start, peer), :]


def core_kernel(heads, place, lengths, bias, kv, *refs):
    count = (len(refs) - 7) // 2
    pieces, returned = refs[:count], refs[count : 2 * count]
    kv_grad, key_all, value_all, query_flat, grad_flat, probs_all, score_all = refs[2 * count :]
    peers, planes, peer, both = kv.shape
    width = both // 2
    rows = peers * peer
    wide = heads * width
    scale = width**-0.5
    plane = place[1]
    for j in range(planes):
        block = kv[:, j].reshape(rows, both)
        key_all[j * rows : (j + 1) * rows, :] = block[:, :width]
        value_all[j * rows : (j + 1) * rows, :] = block[:, width:]
    size = pieces[0].shape[0]
    for index, piece in enumerate(pieces):
        for h in range(heads):
            at = h * rows + index * size
            query_flat[at : at + size, :] = piece[:, h * width : (h + 1) * width]
            grad_flat[at : at + size, :] = piece[:, wide + h * width : wide + (h + 1) * width]
    joined = plane * rows < lengths[0, 0]
    own_bias = bias[...]
    added = []
    for j in range(planes):
        other = jnp.where(joined & (plane > j), 0.0, HIDDEN).astype(jnp.float32)
        added.append(jnp.where(plane == j, own_bias, other))
    added = jnp.concatenate(added, axis=0)
    for h in range(heads):
        own = slice(h * rows, (h + 1) * rows)
        score = contract(key_all[...], query_flat[own, :]) * scale + added
        weight = jnp.exp(score - jnp.max(score, axis=0, keepdims=True))
        probs = weight * (1.0 / jnp.sum(weight, axis=0, keepdims=True))
        prob_grad = contract(value_all[...], grad_flat[own, :])
        delta = jnp.sum(probs * prob_grad, axis=0, keepdims=True)
        probs_all[:, own] = probs.astype(jnp.bfloat16)
        score_all[:, own] = (probs * (prob_grad - delta)).astype(jnp.bfloat16)
    key_grad = (multiply(score_all[...], query_flat[...]) * scale).astype(jnp.bfloat16)
    value_grad = multiply(probs_all[...], grad_flat[...]).astype(jnp.bfloat16)
    for j in range(planes):
        own = slice(j * rows, (j + 1) * rows)
        kv_grad[:, j, :, :width] = key_grad[own].reshape(peers, peer, width)
        kv_grad[:, j, :, width:] = value_grad[own].reshape(peers, peer, width)
    attended = multiply(value_all[...].T, probs_all[...])
    query_grad = multiply(key_all[...].T, score_all[...]) * scale
    for h in range(heads):
        own = slice(h * rows, (h + 1) * rows)
        out = attended[:, own].T.astype(jnp.bfloat16)
        grad = query_grad[:, own].T.astype(jnp.bfloat16)
        for index, piece in enumerate(returned):
            part = slice(index * size, (index + 1) * size)
            piece[:, h * width : (h + 1) * width] = out[part]
            piece[:, wide + h * width : wide + (h + 1) * width] = grad[part]


def unpack_kernel(place, kv, *refs):
    pieces = refs[:-4]
    attended, query_grad, key_grad, value_grad = refs[-4:]
    own = place[0]
    peers, planes, peer, both = kv.shape
    width, wide = both // 2, attended.shape[1]
    size = pieces[0].shape[0]
    for index, piece in enumerate(pieces):
        start = pl.multiple_of(lax.bitwise_xor(own, index) * size, size)
        attended[pl.ds(start, size), :] = piece[:, :wide]
        query_grad[pl.ds(start, size), :] = piece[:, wide:]
    total = kv[:, 0].astype(jnp.float32)
    for j in range(1, planes):
        total = total + kv[:, j].astype(jnp.float32)
    total = total.reshape(peers * peer, both).astype(jnp.bfloat16)
    key_grad[...] = total[:, :width]
    value_grad[...] = total[:, width:]


def local(queries, keys, values, out_grad, doc_lengths, source_slot):
    rows, wide = queries.shape
    width = keys.shape[1]
    heads = wide // width
    peers, planes = lax.axis_size("dp"), lax.axis_size("ctx")
    peer = rows // peers
    swapped = peers == 8 and peer % 16 == 0
    place = jnp.stack([lax.axis_index("dp"), lax.axis_index("ctx")]).astype(jnp.int32)
    low = functools.partial(jax.ShapeDtypeStruct, dtype=jnp.bfloat16)

    kv = jnp.concatenate([keys, values], axis=1).reshape(peers, 1, peer, 2 * width)
    kv = jnp.broadcast_to(kv, (peers, planes, peer, 2 * width))

    def everywhere(x):
        x = x.reshape(peers * planes, peer, 2 * width)
        x = lax.all_to_all(x, ("dp", "ctx"), split_axis=0, concat_axis=0, tiled=True)
        return x.reshape(peers, planes, peer, 2 * width)

    def in_plane(pieces):
        if not swapped:
            return [lax.all_to_all(pieces[0], "dp", split_axis=0, concat_axis=0, tiled=True)]
        return [pieces[0]] + [
            lax.ppermute(pieces[s], "dp", [(i, i ^ s) for i in range(peers)])
            for s in range(1, peers)
        ]

    kv = everywhere(kv)
    if swapped:
        pieces = pl.pallas_call(
            functools.partial(pack_kernel, peer),
            out_shape=[low((peer, 2 * wide))] * peers,
            in_specs=[SMEM, VMEM, VMEM],
            out_specs=[VMEM] * peers,
            compiler_params=params(4),
            name="pack",
        )(place, queries, out_grad)
    else:
        pieces = [jnp.concatenate([queries, out_grad], axis=1)]
    pieces = in_plane(pieces)
    bias = pl.pallas_call(
        functools.partial(mask_kernel, peer, swapped),
        out_shape=jax.ShapeDtypeStruct((rows, rows), jnp.float32),
        in_specs=[SMEM, SMEM, VMEM],
        out_specs=VMEM,
        compiler_params=params(4),
        name="mask",
    )(place, doc_lengths, source_slot.reshape(1, rows))
    fine = peer % 16 == 0
    if not fine:
        kv = kv.transpose(1, 0, 2, 3).reshape(1, planes, rows, 2 * width)
    count = rows * planes
    results = pl.pallas_call(
        functools.partial(core_kernel, heads),
        out_shape=[low(p.shape) for p in pieces] + [low(kv.shape)],
        in_specs=[SMEM, SMEM] + [VMEM] * (2 + len(pieces)),
        out_specs=[VMEM] * (len(pieces) + 1),
        scratch_shapes=[
            pltpu.VMEM((count, width), jnp.bfloat16),
            pltpu.VMEM((count, width), jnp.bfloat16),
            pltpu.VMEM((rows * heads, width), jnp.bfloat16),
            pltpu.VMEM((rows * heads, width), jnp.bfloat16),
            pltpu.VMEM((count, rows * heads), jnp.bfloat16),
            pltpu.VMEM((count, rows * heads), jnp.bfloat16),
        ],
        compiler_params=params(16 if planes <= 4 else 48),
        name="core",
    )(place, doc_lengths, bias, kv, *pieces)
    pieces, kv = list(results[:-1]), results[-1]
    if not fine:
        kv = kv.reshape(planes, peers, peer, 2 * width).transpose(1, 0, 2, 3)
    kv = everywhere(kv)
    if not fine:
        kv = kv.transpose(1, 0, 2, 3).reshape(1, planes, rows, 2 * width)
    pieces = in_plane(pieces)
    return tuple(
        pl.pallas_call(
            unpack_kernel,
            out_shape=[low((rows, wide))] * 2 + [low((rows, width))] * 2,
            in_specs=[SMEM, VMEM] + [VMEM] * len(pieces),
            out_specs=[VMEM] * 4,
            compiler_params=params(8),
            name="unpack",
        )(place if swapped else place * 0, kv, *pieces)
    )


def solution(mesh):
    rows = P(("dp", "ctx"), None)
    return jax.shard_map(
        local,
        mesh=mesh,
        in_specs=(rows, rows, rows, rows, P("dp", None), P(("dp", "ctx"))),
        out_specs=(rows, rows, rows, rows),
        check_vma=False,
    )
```

```python
import functools

import jax
import jax.numpy as jnp
from jax import lax
from jax.experimental import pallas as pl
from jax.experimental.pallas import tpu as pltpu
from jax.sharding import PartitionSpec as P

HIDDEN = -1e30
VMEM = pl.BlockSpec(memory_space=pltpu.VMEM)
SMEM = pl.BlockSpec(memory_space=pltpu.SMEM)
HBM = pl.BlockSpec(memory_space=pltpu.HBM)


def contract(left, right):
    return lax.dot_general(
        left, right, (((1,), (1,)), ((), ())), preferred_element_type=jnp.float32
    )


def multiply(left, right):
    return jnp.dot(left, right, preferred_element_type=jnp.float32)


def params(mib):
    return pltpu.CompilerParams(vmem_limit_bytes=mib * 1024 * 1024)


def low(shape):
    return jax.ShapeDtypeStruct(shape, jnp.bfloat16)


def near(shape):
    return pltpu.VMEM(shape, jnp.bfloat16)


def far(x):
    return pltpu.with_memory_space_constraint(x, pltpu.HBM)


def ordered(blocks):
    if len(blocks) == 1:
        return [blocks[0]]
    first, second = blocks[:-1], blocks[-1]
    return [piece for k, block in enumerate(first) for piece in (block.at[0], second.at[k])]


def parted(blocks):
    if len(blocks) == 1:
        return [blocks[0]]
    return [block.at[core] for block in blocks for core in range(2)]


def fill_bias(peer, swapped, lengths, slot_row, bias):
    rows = slot_row.shape[1]
    own, first = lax.axis_index("dp"), lax.axis_index("ctx") * rows
    slot = jnp.broadcast_to(slot_row[...], (rows, rows))
    along = lax.broadcasted_iota(jnp.int32, (rows, rows), 1)
    down = lax.broadcasted_iota(jnp.int32, (rows, rows), 0)
    key_pos = jnp.sum(jnp.where(slot == down, along, 0), axis=1, keepdims=True)
    slot_down = slot.astype(jnp.float32).T.astype(jnp.int32)
    wanted = lax.bitwise_xor(along // peer, own) * peer + along % peer if swapped else along
    query_pos = jnp.sum(jnp.where(slot_down == wanted, down, 0), axis=0, keepdims=True)

    def later(k, carry):
        end, start = carry
        end = end + lengths[0, k]
        return end, jnp.where(query_pos + first >= end, end, start)

    _, doc_start = lax.fori_loop(
        0, lengths.shape[1], later, (jnp.int32(0), jnp.zeros((1, rows), jnp.int32))
    )
    seen = (key_pos <= query_pos) & (key_pos + first >= doc_start)
    bias[:rows, :] = jnp.where(seen, 0.0, HIDDEN)
    joined = jnp.where(first < lengths[0, 0], 0.0, HIDDEN).astype(jnp.float32)
    bias[rows:, :] = jnp.full((bias.shape[0] - rows, rows), joined)


def pack_kernel(keys, values, queries, out_grad, lengths, slot_row, *refs):
    *pieces, bias, kv, kv_buf, query_buf, grad_buf, length_buf, slot_buf, sems = refs
    own = lax.axis_index("dp")
    wide, width = queries.shape[1], keys.shape[2]
    peers, planes, peer, _ = kv.shape
    come = [
        pltpu.make_async_copy(keys, kv_buf.at[:, :, :width], sems.at[0]),
        pltpu.make_async_copy(values, kv_buf.at[:, :, width:], sems.at[1]),
        pltpu.make_async_copy(queries, query_buf, sems.at[2]),
        pltpu.make_async_copy(out_grad, grad_buf, sems.at[3]),
        pltpu.make_async_copy(lengths, length_buf, sems.at[4]),
        pltpu.make_async_copy(slot_row, slot_buf, sems.at[5]),
    ]
    for copy in come:
        copy.start()
    come[0].wait()
    come[1].wait()
    leave = [pltpu.make_async_copy(kv_buf, kv.at[:, j], sems.at[6 + j]) for j in range(planes)]
    for copy in leave:
        copy.start()
    come[4].wait()
    come[5].wait()
    fill_bias(peer, True, length_buf, slot_buf, bias)
    for k, buf in enumerate((query_buf, grad_buf)):
        come[2 + k].wait()
        for index, piece in enumerate(parted(pieces)):
            start = pl.multiple_of(lax.bitwise_xor(own, index) * peer, peer)
            piece[:, k * wide : (k + 1) * wide] = buf[pl.ds(start, peer), :]
    for copy in leave:
        copy.wait()


def join_kernel(*refs):
    *blocks, out = refs
    for k, block in enumerate(blocks):
        out[k] = block[1]


def core_kernel(heads, taken, bias, kv, *refs):
    pieces = ordered(refs[:taken])
    *returned, kv_grad, key_all, value_all, query_flat, grad_flat, probs_all, score_all = refs[
        taken:-2
    ]
    grad_buf, sem = refs[-2:]
    returned = parted(returned)
    peers, planes, peer, both = kv.shape
    width = both // 2
    rows = peers * peer
    wide = heads * width
    scale = width**-0.5
    plane = lax.axis_index("ctx")
    for j in range(planes):
        block = kv[:, j].reshape(rows, both)
        key_all[j * rows : (j + 1) * rows, :] = block[:, :width]
        value_all[j * rows : (j + 1) * rows, :] = block[:, width:]
    size = pieces[0].shape[0]
    for index, piece in enumerate(pieces):
        for h in range(heads):
            at = h * rows + index * size
            query_flat[at : at + size, :] = piece[:, h * width : (h + 1) * width]
            grad_flat[at : at + size, :] = piece[:, wide + h * width : wide + (h + 1) * width]
    seen, before = bias[:rows, :], bias[rows : rows + 1, :]
    added = []
    for j in range(planes):
        other = jnp.where(plane > j, before, HIDDEN)
        added.append(jnp.where(plane == j, seen, other))
    added = jnp.concatenate(added, axis=0)
    for h in range(heads):
        own = slice(h * rows, (h + 1) * rows)
        score = contract(key_all[...], query_flat[own, :]) * scale + added
        weight = jnp.exp(score - jnp.max(score, axis=0, keepdims=True))
        probs = weight * (1.0 / jnp.sum(weight, axis=0, keepdims=True))
        prob_grad = contract(value_all[...], grad_flat[own, :])
        delta = jnp.sum(probs * prob_grad, axis=0, keepdims=True)
        probs_all[:, own] = probs.astype(jnp.bfloat16)
        score_all[:, own] = (probs * (prob_grad - delta)).astype(jnp.bfloat16)
    key_grad = (multiply(score_all[...], query_flat[...]) * scale).astype(jnp.bfloat16)
    value_grad = multiply(probs_all[...], grad_flat[...]).astype(jnp.bfloat16)
    for j in range(planes):
        own = slice(j * rows, (j + 1) * rows)
        grad_buf[:, j, :, :width] = key_grad[own].reshape(peers, peer, width)
        grad_buf[:, j, :, width:] = value_grad[own].reshape(peers, peer, width)
    leave = pltpu.make_async_copy(grad_buf, kv_grad, sem)
    leave.start()
    attended = multiply(value_all[...].T, probs_all[...]).astype(jnp.bfloat16)
    query_grad = (multiply(key_all[...].T, score_all[...]) * scale).astype(jnp.bfloat16)
    for k, source in enumerate((attended, query_grad)):
        for h in range(heads):
            turned = source[:, h * rows : (h + 1) * rows].T
            at = (k * heads + h) * width
            for index, piece in enumerate(returned):
                piece[:, at : at + width] = turned[index * size : (index + 1) * size]
    leave.wait()


def last_kernel(kv, *refs):
    *blocks, attended, query_grad, key_grad, value_grad, key_buf, value_buf, sems = refs
    pieces = ordered(blocks)
    wide, size = attended.shape[1], pieces[0].shape[0]
    own = lax.axis_index("dp") if len(pieces) > 1 else 0
    copies = []
    for index, piece in enumerate(pieces):
        start = pl.multiple_of(lax.bitwise_xor(own, index) * size, size)
        for k, target in enumerate((attended, query_grad)):
            copies.append(
                pltpu.make_async_copy(
                    piece.at[:, k * wide : (k + 1) * wide],
                    target.at[pl.ds(start, size), :],
                    sems.at[len(copies)],
                )
            )
            copies[-1].start()
    peers, planes, peer, both = kv.shape
    width = both // 2
    for k, (buf, target) in enumerate(((key_buf, key_grad), (value_buf, value_grad))):
        part = slice(k * width, (k + 1) * width)
        total = kv[:, 0, :, part].astype(jnp.float32)
        for j in range(1, planes):
            total = total + kv[:, j, :, part].astype(jnp.float32)
        buf[...] = total.reshape(peers * peer, width).astype(jnp.bfloat16)
        copies.append(pltpu.make_async_copy(buf, target, sems.at[len(copies)]))
        copies[-1].start()
    for copy in copies:
        copy.wait()


def local(queries, keys, values, out_grad, doc_lengths, source_slot):
    rows, wide = queries.shape
    width = keys.shape[1]
    heads = wide // width
    peers, planes = lax.axis_size("dp"), lax.axis_size("ctx")
    peer = rows // peers
    fine = peer % 16 == 0
    swapped = peers == 8 and fine
    kv_shape = (peers, planes, peer, 2 * width)

    def everywhere(x):
        x = x.reshape(peers * planes, peer, 2 * width)
        x = lax.all_to_all(x, ("dp", "ctx"), split_axis=0, concat_axis=0, tiled=True)
        return x.reshape(kv_shape)

    def in_plane(pieces):
        if not swapped:
            return [lax.all_to_all(pieces[0], "dp", split_axis=0, concat_axis=0, tiled=True)]
        came = [pieces[0]] + [
            lax.ppermute(pieces[s], "dp", [(i, i ^ (2 * s)) for i in range(peers)])
            for s in range(1, peers // 2)
        ]
        other = pl.pallas_call(
            join_kernel,
            out_shape=near((peers // 2, peer, 2 * wide)),
            in_specs=[VMEM] * len(came),
            out_specs=VMEM,
            compiler_params=params(4),
            name="join",
        )(*came)
        return came + [lax.ppermute(other, "dp", [(i, i ^ 1) for i in range(peers)])]

    slot_row = source_slot.reshape(1, rows)
    if swapped:
        sent = [near((2, peer, 2 * wide))] * (peers // 2)
        *pieces, bias, kv = pl.pallas_call(
            pack_kernel,
            out_shape=sent + [pltpu.VMEM((rows + 8, rows), jnp.float32), low(kv_shape)],
            in_specs=[HBM] * 6,
            out_specs=[VMEM] * (len(sent) + 1) + [HBM],
            scratch_shapes=[
                pltpu.VMEM((peers, peer, 2 * width), jnp.bfloat16),
                pltpu.VMEM((rows, wide), jnp.bfloat16),
                pltpu.VMEM((rows, wide), jnp.bfloat16),
                pltpu.SMEM(doc_lengths.shape, jnp.int32),
                pltpu.VMEM(slot_row.shape, jnp.int32),
                pltpu.SemaphoreType.DMA((6 + planes,)),
            ],
            compiler_params=params(4),
            name="pack",
        )(
            far(keys.reshape(peers, peer, width)),
            far(values.reshape(peers, peer, width)),
            far(queries),
            far(out_grad),
            far(doc_lengths),
            far(slot_row),
        )
    else:
        sent = [low((rows, 2 * wide))]
        kv = jnp.concatenate([keys, values], axis=1).reshape(peers, 1, peer, 2 * width)
        kv = jnp.broadcast_to(kv, kv_shape)
        pieces = [jnp.concatenate([queries, out_grad], axis=1)]
        bias = pl.pallas_call(
            functools.partial(fill_bias, peer, False),
            out_shape=jax.ShapeDtypeStruct((rows + 8, rows), jnp.float32),
            in_specs=[SMEM, VMEM],
            out_specs=VMEM,
            compiler_params=params(4),
            name="mask",
        )(doc_lengths, slot_row)
    kv = everywhere(kv)
    pieces = in_plane(pieces)
    if not fine:
        kv = kv.transpose(1, 0, 2, 3).reshape(1, planes, rows, 2 * width)
    count = rows * planes
    *pieces, kv = pl.pallas_call(
        functools.partial(core_kernel, heads, len(pieces)),
        out_shape=sent + [low(kv.shape)],
        in_specs=[VMEM] * (2 + len(pieces)),
        out_specs=[VMEM] * len(sent) + [HBM],
        scratch_shapes=[
            pltpu.VMEM((count, width), jnp.bfloat16),
            pltpu.VMEM((count, width), jnp.bfloat16),
            pltpu.VMEM((rows * heads, width), jnp.bfloat16),
            pltpu.VMEM((rows * heads, width), jnp.bfloat16),
            pltpu.VMEM((count, rows * heads), jnp.bfloat16),
            pltpu.VMEM((count, rows * heads), jnp.bfloat16),
            pltpu.VMEM(kv.shape, jnp.bfloat16),
            pltpu.SemaphoreType.DMA,
        ],
        compiler_params=params(16 if planes <= 4 else 48),
        name="core",
    )(bias, kv, *pieces)
    if not fine:
        kv = kv.reshape(planes, peers, peer, 2 * width).transpose(1, 0, 2, 3)
    kv = everywhere(kv)
    if not fine:
        kv = kv.transpose(1, 0, 2, 3).reshape(1, planes, rows, 2 * width)
    pieces = in_plane(pieces)
    count = 8 * 2 if swapped else 2
    return tuple(
        pl.pallas_call(
            last_kernel,
            out_shape=[low((rows, wide))] * 2 + [low((rows, width))] * 2,
            in_specs=[VMEM] * (1 + len(pieces)),
            out_specs=[HBM] * 4,
            scratch_shapes=[
                pltpu.VMEM((rows, width), jnp.bfloat16),
                pltpu.VMEM((rows, width), jnp.bfloat16),
                pltpu.SemaphoreType.DMA((count + 2,)),
            ],
            compiler_params=params(8),
            name="last",
        )(kv, *pieces)
    )


def solution(mesh):
    rows = P(("dp", "ctx"), None)
    return jax.shard_map(
        local,
        mesh=mesh,
        in_specs=(rows, rows, rows, rows, P("dp", None), P(("dp", "ctx"))),
        out_specs=(rows, rows, rows, rows),
        check_vma=False,
    )
```

```python
import functools

import jax
import jax.numpy as jnp
from jax import lax
from jax.experimental import pallas as pl
from jax.experimental.pallas import tpu as pltpu
from jax.sharding import PartitionSpec as P

HIDDEN = -1e30
VMEM = pl.BlockSpec(memory_space=pltpu.VMEM)
SMEM = pl.BlockSpec(memory_space=pltpu.SMEM)
HBM = pl.BlockSpec(memory_space=pltpu.HBM)


def contract(left, right):
    return lax.dot_general(
        left, right, (((1,), (1,)), ((), ())), preferred_element_type=jnp.float32
    )


def multiply(left, right):
    return jnp.dot(left, right, preferred_element_type=jnp.float32)


def params(mib):
    return pltpu.CompilerParams(vmem_limit_bytes=mib * 1024 * 1024)


def low(shape):
    return jax.ShapeDtypeStruct(shape, jnp.bfloat16)


def near(shape):
    return pltpu.VMEM(shape, jnp.bfloat16)


def far(x):
    return pltpu.with_memory_space_constraint(x, pltpu.HBM)


def parted(blocks):
    if len(blocks) == 1:
        return [blocks[0]]
    kept, crossed = blocks
    return [half.at[k] for k in range(kept.shape[0]) for half in (kept, crossed)]


def paired(blocks):
    if len(blocks) == 1:
        return [blocks[0]]
    kept, swapped, *chips = blocks
    return [kept.at[0], swapped.at[0]] + [chip.at[core] for chip in chips for core in range(2)]


def fill_bias(peer, swapped, lengths, slot_row, bias):
    rows = slot_row.shape[1]
    own, first = lax.axis_index("dp"), lax.axis_index("ctx") * rows
    slot = jnp.broadcast_to(slot_row[...], (rows, rows))
    along = lax.broadcasted_iota(jnp.int32, (rows, rows), 1)
    down = lax.broadcasted_iota(jnp.int32, (rows, rows), 0)
    key_pos = jnp.sum(jnp.where(slot == down, along, 0), axis=1, keepdims=True)
    slot_down = slot.astype(jnp.float32).T.astype(jnp.int32)
    wanted = lax.bitwise_xor(along // peer, own) * peer + along % peer if swapped else along
    query_pos = jnp.sum(jnp.where(slot_down == wanted, down, 0), axis=0, keepdims=True)

    def later(k, carry):
        end, start = carry
        end = end + lengths[0, k]
        return end, jnp.where(query_pos + first >= end, end, start)

    _, doc_start = lax.fori_loop(
        0, lengths.shape[1], later, (jnp.int32(0), jnp.zeros((1, rows), jnp.int32))
    )
    seen = (key_pos <= query_pos) & (key_pos + first >= doc_start)
    bias[:rows, :] = jnp.where(seen, 0.0, HIDDEN)
    joined = jnp.where(first < lengths[0, 0], 0.0, HIDDEN).astype(jnp.float32)
    bias[rows:, :] = jnp.full((bias.shape[0] - rows, rows), joined)


def pack_kernel(keys, values, queries, out_grad, lengths, slot_row, *refs):
    kept, crossed, bias, kv, kv_buf, query_buf, grad_buf, length_buf, slot_buf, sems = refs
    own = lax.axis_index("dp")
    wide, width = queries.shape[1], keys.shape[2]
    peers, planes, peer, _ = kv.shape
    come = [
        pltpu.make_async_copy(keys, kv_buf.at[:, :, :width], sems.at[0]),
        pltpu.make_async_copy(values, kv_buf.at[:, :, width:], sems.at[1]),
        pltpu.make_async_copy(queries, query_buf, sems.at[2]),
        pltpu.make_async_copy(out_grad, grad_buf, sems.at[3]),
        pltpu.make_async_copy(lengths, length_buf, sems.at[4]),
        pltpu.make_async_copy(slot_row, slot_buf, sems.at[5]),
    ]
    for copy in come:
        copy.start()
    come[0].wait()
    come[1].wait()
    leave = [pltpu.make_async_copy(kv_buf, kv.at[:, j], sems.at[6 + j]) for j in range(planes)]
    for copy in leave:
        copy.start()
    come[4].wait()
    come[5].wait()
    fill_bias(peer, True, length_buf, slot_buf, bias)
    for k, buf in enumerate((query_buf, grad_buf)):
        come[2 + k].wait()
        for index, piece in enumerate(parted((kept, crossed))):
            start = pl.multiple_of(lax.bitwise_xor(own, index) * peer, peer)
            piece[:, k * wide : (k + 1) * wide] = buf[pl.ds(start, peer), :]
    for copy in leave:
        copy.wait()


def pair_kernel(kept, swapped, *out):
    for k, block in enumerate(out):
        block[0] = kept[k + 1]
        block[1] = swapped[k + 1]


def core_kernel(heads, taken, bias, kv, *refs):
    pieces = paired(refs[:taken])
    *returned, kv_grad, key_all, value_all, query_flat, grad_flat, probs_all, score_all = refs[
        taken:-2
    ]
    grad_buf, sem = refs[-2:]
    returned = parted(returned)
    peers, planes, peer, both = kv.shape
    width = both // 2
    rows = peers * peer
    wide = heads * width
    scale = width**-0.5
    plane = lax.axis_index("ctx")
    for j in range(planes):
        block = kv[:, j].reshape(rows, both)
        key_all[j * rows : (j + 1) * rows, :] = block[:, :width]
        value_all[j * rows : (j + 1) * rows, :] = block[:, width:]
    size = pieces[0].shape[0]
    for index, piece in enumerate(pieces):
        for h in range(heads):
            at = h * rows + index * size
            query_flat[at : at + size, :] = piece[:, h * width : (h + 1) * width]
            grad_flat[at : at + size, :] = piece[:, wide + h * width : wide + (h + 1) * width]
    seen, before = bias[:rows, :], bias[rows : rows + 1, :]
    added = []
    for j in range(planes):
        other = jnp.where(plane > j, before, HIDDEN)
        added.append(jnp.where(plane == j, seen, other))
    added = jnp.concatenate(added, axis=0)
    for h in range(heads):
        own = slice(h * rows, (h + 1) * rows)
        score = contract(key_all[...], query_flat[own, :]) * scale + added
        weight = jnp.exp(score - jnp.max(score, axis=0, keepdims=True))
        probs = weight * (1.0 / jnp.sum(weight, axis=0, keepdims=True))
        prob_grad = contract(value_all[...], grad_flat[own, :])
        delta = jnp.sum(probs * prob_grad, axis=0, keepdims=True)
        probs_all[:, own] = probs.astype(jnp.bfloat16)
        score_all[:, own] = (probs * (prob_grad - delta)).astype(jnp.bfloat16)
    key_grad = (multiply(score_all[...], query_flat[...]) * scale).astype(jnp.bfloat16)
    value_grad = multiply(probs_all[...], grad_flat[...]).astype(jnp.bfloat16)
    for j in range(planes):
        own = slice(j * rows, (j + 1) * rows)
        grad_buf[:, j, :, :width] = key_grad[own].reshape(peers, peer, width)
        grad_buf[:, j, :, width:] = value_grad[own].reshape(peers, peer, width)
    leave = pltpu.make_async_copy(grad_buf, kv_grad, sem)
    leave.start()
    attended = multiply(value_all[...].T, probs_all[...]).astype(jnp.bfloat16)
    query_grad = (multiply(key_all[...].T, score_all[...]) * scale).astype(jnp.bfloat16)
    for k, source in enumerate((attended, query_grad)):
        for h in range(heads):
            turned = source[:, h * rows : (h + 1) * rows].T
            at = (k * heads + h) * width
            for index, piece in enumerate(returned):
                piece[:, at : at + width] = turned[index * size : (index + 1) * size]
    leave.wait()


def last_kernel(kv, *refs):
    *blocks, attended, query_grad, key_grad, value_grad, key_buf, value_buf, sems = refs
    pieces = paired(blocks)
    wide, size = attended.shape[1], pieces[0].shape[0]
    own = lax.axis_index("dp") if len(pieces) > 1 else 0
    copies = []
    for index, piece in enumerate(pieces):
        start = pl.multiple_of(lax.bitwise_xor(own, index) * size, size)
        for k, target in enumerate((attended, query_grad)):
            copies.append(
                pltpu.make_async_copy(
                    piece.at[:, k * wide : (k + 1) * wide],
                    target.at[pl.ds(start, size), :],
                    sems.at[len(copies)],
                )
            )
            copies[-1].start()
    peers, planes, peer, both = kv.shape
    width = both // 2
    for k, (buf, target) in enumerate(((key_buf, key_grad), (value_buf, value_grad))):
        part = slice(k * width, (k + 1) * width)
        total = kv[:, 0, :, part].astype(jnp.float32)
        for j in range(1, planes):
            total = total + kv[:, j, :, part].astype(jnp.float32)
        buf[...] = total.reshape(peers * peer, width).astype(jnp.bfloat16)
        copies.append(pltpu.make_async_copy(buf, target, sems.at[len(copies)]))
        copies[-1].start()
    for copy in copies:
        copy.wait()


def local(queries, keys, values, out_grad, doc_lengths, source_slot):
    rows, wide = queries.shape
    width = keys.shape[1]
    heads = wide // width
    peers, planes = lax.axis_size("dp"), lax.axis_size("ctx")
    peer = rows // peers
    fine = peer % 16 == 0
    swapped = peers == 8 and fine
    kv_shape = (peers, planes, peer, 2 * width)

    def everywhere(x):
        x = x.reshape(peers * planes, peer, 2 * width)
        x = lax.all_to_all(x, ("dp", "ctx"), split_axis=0, concat_axis=0, tiled=True)
        return x.reshape(kv_shape)

    def swap(x, mask):
        return lax.ppermute(x, "dp", [(i, i ^ mask) for i in range(peers)])

    def in_plane(pieces):
        if not swapped:
            return [lax.all_to_all(pieces[0], "dp", split_axis=0, concat_axis=0, tiled=True)]
        kept, crossed = pieces
        crossed = swap(crossed, 1)
        chips = pl.pallas_call(
            pair_kernel,
            out_shape=[near((2, peer, 2 * wide))] * (peers // 2 - 1),
            in_specs=[VMEM] * 2,
            out_specs=[VMEM] * (peers // 2 - 1),
            compiler_params=params(4),
            name="pair",
        )(kept, crossed)
        return [kept, crossed] + [swap(chip, 2 * s + 2) for s, chip in enumerate(chips)]

    slot_row = source_slot.reshape(1, rows)
    if swapped:
        sent = [near((peers // 2, peer, 2 * wide))] * 2
        *pieces, bias, kv = pl.pallas_call(
            pack_kernel,
            out_shape=sent + [pltpu.VMEM((rows + 8, rows), jnp.float32), low(kv_shape)],
            in_specs=[HBM] * 6,
            out_specs=[VMEM] * 3 + [HBM],
            scratch_shapes=[
                pltpu.VMEM((peers, peer, 2 * width), jnp.bfloat16),
                pltpu.VMEM((rows, wide), jnp.bfloat16),
                pltpu.VMEM((rows, wide), jnp.bfloat16),
                pltpu.SMEM(doc_lengths.shape, jnp.int32),
                pltpu.VMEM(slot_row.shape, jnp.int32),
                pltpu.SemaphoreType.DMA((6 + planes,)),
            ],
            compiler_params=params(4),
            name="pack",
        )(
            far(keys.reshape(peers, peer, width)),
            far(values.reshape(peers, peer, width)),
            far(queries),
            far(out_grad),
            far(doc_lengths),
            far(slot_row),
        )
    else:
        sent = [low((rows, 2 * wide))]
        kv = jnp.concatenate([keys, values], axis=1).reshape(peers, 1, peer, 2 * width)
        kv = jnp.broadcast_to(kv, kv_shape)
        pieces = [jnp.concatenate([queries, out_grad], axis=1)]
        bias = pl.pallas_call(
            functools.partial(fill_bias, peer, False),
            out_shape=jax.ShapeDtypeStruct((rows + 8, rows), jnp.float32),
            in_specs=[SMEM, VMEM],
            out_specs=VMEM,
            compiler_params=params(4),
            name="mask",
        )(doc_lengths, slot_row)
    kv = everywhere(kv)
    pieces = in_plane(pieces)
    if not fine:
        kv = kv.transpose(1, 0, 2, 3).reshape(1, planes, rows, 2 * width)
    count = rows * planes
    *pieces, kv = pl.pallas_call(
        functools.partial(core_kernel, heads, len(pieces)),
        out_shape=sent + [low(kv.shape)],
        in_specs=[VMEM] * (2 + len(pieces)),
        out_specs=[VMEM] * len(sent) + [HBM],
        scratch_shapes=[
            pltpu.VMEM((count, width), jnp.bfloat16),
            pltpu.VMEM((count, width), jnp.bfloat16),
            pltpu.VMEM((rows * heads, width), jnp.bfloat16),
            pltpu.VMEM((rows * heads, width), jnp.bfloat16),
            pltpu.VMEM((count, rows * heads), jnp.bfloat16),
            pltpu.VMEM((count, rows * heads), jnp.bfloat16),
            pltpu.VMEM(kv.shape, jnp.bfloat16),
            pltpu.SemaphoreType.DMA,
        ],
        compiler_params=params(16 if planes <= 4 else 48),
        name="core",
    )(bias, kv, *pieces)
    if not fine:
        kv = kv.reshape(planes, peers, peer, 2 * width).transpose(1, 0, 2, 3)
    kv = everywhere(kv)
    if not fine:
        kv = kv.transpose(1, 0, 2, 3).reshape(1, planes, rows, 2 * width)
    pieces = in_plane(pieces)
    count = 8 * 2 if swapped else 2
    return tuple(
        pl.pallas_call(
            last_kernel,
            out_shape=[low((rows, wide))] * 2 + [low((rows, width))] * 2,
            in_specs=[VMEM] * (1 + len(pieces)),
            out_specs=[HBM] * 4,
            scratch_shapes=[
                pltpu.VMEM((rows, width), jnp.bfloat16),
                pltpu.VMEM((rows, width), jnp.bfloat16),
                pltpu.SemaphoreType.DMA((count + 2,)),
            ],
            compiler_params=params(8),
            name="last",
        )(kv, *pieces)
    )


def solution(mesh):
    rows = P(("dp", "ctx"), None)
    return jax.shard_map(
        local,
        mesh=mesh,
        in_specs=(rows, rows, rows, rows, P("dp", None), P(("dp", "ctx"))),
        out_specs=(rows, rows, rows, rows),
        check_vma=False,
    )
```

```python
import functools
import math

import jax
import jax.numpy as jnp
from jax import lax
from jax.experimental import pallas as pl
from jax.experimental.pallas import tpu as pltpu
from jax.sharding import PartitionSpec as P

HIDDEN = -1e30
VMEM = pl.BlockSpec(memory_space=pltpu.VMEM)
SMEM = pl.BlockSpec(memory_space=pltpu.SMEM)
HBM = pl.BlockSpec(memory_space=pltpu.HBM)


def contract(left, right):
    return lax.dot_general(
        left, right, (((1,), (1,)), ((), ())), preferred_element_type=jnp.float32
    )


def multiply(left, right):
    return jnp.dot(left, right, preferred_element_type=jnp.float32)


def params(mib):
    return pltpu.CompilerParams(vmem_limit_bytes=mib * 1024 * 1024)


def low(shape):
    return jax.ShapeDtypeStruct(shape, jnp.bfloat16)


def near(shape):
    return pltpu.VMEM(shape, jnp.bfloat16)


def far(x):
    return pltpu.with_memory_space_constraint(x, pltpu.HBM)


def parted(blocks):
    if len(blocks) == 1:
        return [blocks[0]]
    kept, crossed = blocks
    return [half.at[k] for k in range(kept.shape[0]) for half in (kept, crossed)]


def paired(blocks):
    if len(blocks) == 1:
        return [blocks[0]]
    kept, swapped, *chips = blocks
    return [kept.at[0], swapped.at[0]] + [chip.at[core] for chip in chips for core in range(2)]


def fill_bias(peer, swapped, lengths, slot_row, bias):
    rows = slot_row.shape[1]
    own, first = lax.axis_index("dp"), lax.axis_index("ctx") * rows
    slot = jnp.broadcast_to(slot_row[...], (rows, rows))
    along = lax.broadcasted_iota(jnp.int32, (rows, rows), 1)
    down = lax.broadcasted_iota(jnp.int32, (rows, rows), 0)
    key_pos = jnp.sum(jnp.where(slot == down, along, 0), axis=1, keepdims=True)
    slot_down = slot.astype(jnp.float32).T.astype(jnp.int32)
    wanted = lax.bitwise_xor(along // peer, own) * peer + along % peer if swapped else along
    query_pos = jnp.sum(jnp.where(slot_down == wanted, down, 0), axis=0, keepdims=True)

    def later(k, carry):
        end, start = carry
        end = end + lengths[0, k]
        return end, jnp.where(query_pos + first >= end, end, start)

    _, doc_start = lax.fori_loop(
        0, lengths.shape[1], later, (jnp.int32(0), jnp.zeros((1, rows), jnp.int32))
    )
    seen = (key_pos <= query_pos) & (key_pos + first >= doc_start)
    bias[:rows, :] = jnp.where(seen, 0.0, HIDDEN)
    joined = jnp.where(first < lengths[0, 0], 0.0, HIDDEN).astype(jnp.float32)
    bias[rows:, :] = jnp.full((bias.shape[0] - rows, rows), joined)


def pack_kernel(keys, values, queries, out_grad, lengths, slot_row, *refs):
    kept, crossed, bias, kv, kv_buf, query_buf, grad_buf, length_buf, slot_buf, sems = refs
    own = lax.axis_index("dp")
    wide, width = queries.shape[1], keys.shape[2]
    peers, planes, peer, _ = kv.shape
    come = [
        pltpu.make_async_copy(keys, kv_buf.at[:, :, :width], sems.at[0]),
        pltpu.make_async_copy(values, kv_buf.at[:, :, width:], sems.at[1]),
        pltpu.make_async_copy(queries, query_buf, sems.at[2]),
        pltpu.make_async_copy(out_grad, grad_buf, sems.at[3]),
        pltpu.make_async_copy(lengths, length_buf, sems.at[4]),
        pltpu.make_async_copy(slot_row, slot_buf, sems.at[5]),
    ]
    for copy in come:
        copy.start()
    come[0].wait()
    come[1].wait()
    leave = [pltpu.make_async_copy(kv_buf, kv.at[:, j], sems.at[6 + j]) for j in range(planes)]
    for copy in leave:
        copy.start()
    come[4].wait()
    come[5].wait()
    fill_bias(peer, True, length_buf, slot_buf, bias)
    for k, buf in enumerate((query_buf, grad_buf)):
        come[2 + k].wait()
        for index, piece in enumerate(parted((kept, crossed))):
            start = pl.multiple_of(lax.bitwise_xor(own, index) * peer, peer)
            piece[:, k * wide : (k + 1) * wide] = buf[pl.ds(start, peer), :]
    for copy in leave:
        copy.wait()


def pair_kernel(kept, swapped, *out):
    for k, block in enumerate(out):
        block[0] = kept[k + 1]
        block[1] = swapped[k + 1]


def core_kernel(heads, taken, bias, kv, *refs):
    planes, plane = kv.shape[1], lax.axis_index("ctx")
    if planes > 4:
        core(heads, taken, None, bias, kv, *refs)
        return
    for k in range(planes):
        pl.when(plane == k)(functools.partial(core, heads, taken, k, bias, kv, *refs))


def core(heads, taken, plane, bias, kv, *refs):
    pieces = paired(refs[:taken])
    *returned, kv_grad, key_all, value_all, query_flat, grad_flat, probs_all, score_all = refs[
        taken:-2
    ]
    grad_buf, sem = refs[-2:]
    returned = parted(returned)
    peers, planes, peer, both = kv.shape
    width = both // 2
    rows = peers * peer
    wide = heads * width
    scale = width**-0.5
    seen, before = bias[:rows, :], bias[rows : rows + 1, :]
    added = []
    for j in range(planes if plane is None else plane + 1):
        if plane is None:
            other = jnp.where(lax.axis_index("ctx") > j, before, HIDDEN)
            added.append(jnp.where(lax.axis_index("ctx") == j, seen, other))
        else:
            added.append(seen if j == plane else jnp.broadcast_to(before, (rows, rows)))
        block = kv[:, j].reshape(rows, both)
        key_all[j * rows : (j + 1) * rows, :] = block[:, :width]
        value_all[j * rows : (j + 1) * rows, :] = block[:, width:]
    count = len(added) * rows
    added = jnp.concatenate(added, axis=0)
    size = pieces[0].shape[0]
    for index, piece in enumerate(pieces):
        for h in range(heads):
            at = h * rows + index * size
            query_flat[at : at + size, :] = piece[:, h * width : (h + 1) * width]
            grad_flat[at : at + size, :] = piece[:, wide + h * width : wide + (h + 1) * width]
    at_once = 2 if heads % 2 == 0 else 1
    added = jnp.concatenate([added] * at_once, axis=1)
    for h in range(0, heads, at_once):
        own = slice(h * rows, (h + at_once) * rows)
        score = contract(key_all[:count], query_flat[own, :]) * (scale * math.log2(math.e)) + added
        weight = jnp.exp2(score - jnp.max(score, axis=0, keepdims=True))
        probs = weight * (1.0 / jnp.sum(weight, axis=0, keepdims=True))
        prob_grad = contract(value_all[:count], grad_flat[own, :])
        delta = jnp.sum(probs * prob_grad, axis=0, keepdims=True)
        probs_all[:count, own] = probs.astype(jnp.bfloat16)
        score_all[:count, own] = (probs * (prob_grad - delta)).astype(jnp.bfloat16)
    key_grad = (multiply(score_all[:count], query_flat[...]) * scale).astype(jnp.bfloat16)
    value_grad = multiply(probs_all[:count], grad_flat[...]).astype(jnp.bfloat16)
    for j in range(planes):
        own = slice(j * rows, (j + 1) * rows)
        if j * rows < count:
            grad_buf[:, j, :, :width] = key_grad[own].reshape(peers, peer, width)
            grad_buf[:, j, :, width:] = value_grad[own].reshape(peers, peer, width)
        else:
            grad_buf[:, j] = jnp.zeros((peers, peer, both), jnp.bfloat16)
    leave = pltpu.make_async_copy(grad_buf, kv_grad, sem)
    leave.start()
    attended = multiply(value_all[:count].T, probs_all[:count]).astype(jnp.bfloat16)
    query_grad = (multiply(key_all[:count].T, score_all[:count]) * scale).astype(jnp.bfloat16)
    for k, source in enumerate((attended, query_grad)):
        for h in range(heads):
            turned = source[:, h * rows : (h + 1) * rows].T
            at = (k * heads + h) * width
            for index, piece in enumerate(returned):
                piece[:, at : at + width] = turned[index * size : (index + 1) * size]
    leave.wait()


def last_kernel(kv, *refs):
    *blocks, attended, query_grad, key_grad, value_grad, key_buf, value_buf, sems = refs
    pieces = paired(blocks)
    wide, size = attended.shape[1], pieces[0].shape[0]
    own = lax.axis_index("dp") if len(pieces) > 1 else 0
    copies = []
    for index, piece in enumerate(pieces):
        start = pl.multiple_of(lax.bitwise_xor(own, index) * size, size)
        for k, target in enumerate((attended, query_grad)):
            copies.append(
                pltpu.make_async_copy(
                    piece.at[:, k * wide : (k + 1) * wide],
                    target.at[pl.ds(start, size), :],
                    sems.at[len(copies)],
                )
            )
            copies[-1].start()
    peers, planes, peer, both = kv.shape
    width = both // 2
    for k, (buf, target) in enumerate(((key_buf, key_grad), (value_buf, value_grad))):
        part = slice(k * width, (k + 1) * width)
        total = kv[:, 0, :, part].astype(jnp.float32)
        for j in range(1, planes):
            total = total + kv[:, j, :, part].astype(jnp.float32)
        buf[...] = total.reshape(peers * peer, width).astype(jnp.bfloat16)
        copies.append(pltpu.make_async_copy(buf, target, sems.at[len(copies)]))
        copies[-1].start()
    for copy in copies:
        copy.wait()


def local(queries, keys, values, out_grad, doc_lengths, source_slot):
    rows, wide = queries.shape
    width = keys.shape[1]
    heads = wide // width
    peers, planes = lax.axis_size("dp"), lax.axis_size("ctx")
    peer = rows // peers
    fine = peer % 16 == 0
    swapped = peers == 8 and fine
    kv_shape = (peers, planes, peer, 2 * width)

    def everywhere(x):
        x = x.reshape(peers * planes, peer, 2 * width)
        x = lax.all_to_all(x, ("dp", "ctx"), split_axis=0, concat_axis=0, tiled=True)
        return x.reshape(kv_shape)

    def swap(x, mask):
        return lax.ppermute(x, "dp", [(i, i ^ mask) for i in range(peers)])

    def in_plane(pieces, cost=None):
        if not swapped:
            return [lax.all_to_all(pieces[0], "dp", split_axis=0, concat_axis=0, tiled=True)]
        kept, crossed = pieces
        crossed = swap(crossed, 1)
        chips = pl.pallas_call(
            pair_kernel,
            out_shape=[near((2, peer, 2 * wide))] * (peers // 2 - 1),
            in_specs=[VMEM] * 2,
            out_specs=[VMEM] * (peers // 2 - 1),
            compiler_params=params(4),
            cost_estimate=cost,
            name="pair",
        )(kept, crossed)
        return [kept, crossed] + [swap(chip, 2 * s + 2) for s, chip in enumerate(chips)]

    slot_row = source_slot.reshape(1, rows)
    if swapped:
        sent = [near((peers // 2, peer, 2 * wide))] * 2
        *pieces, bias, kv = pl.pallas_call(
            pack_kernel,
            out_shape=sent + [pltpu.VMEM((rows + 8, rows), jnp.float32), low(kv_shape)],
            in_specs=[HBM] * 6,
            out_specs=[VMEM] * 3 + [HBM],
            scratch_shapes=[
                pltpu.VMEM((peers, peer, 2 * width), jnp.bfloat16),
                pltpu.VMEM((rows, wide), jnp.bfloat16),
                pltpu.VMEM((rows, wide), jnp.bfloat16),
                pltpu.SMEM(doc_lengths.shape, jnp.int32),
                pltpu.VMEM(slot_row.shape, jnp.int32),
                pltpu.SemaphoreType.DMA((6 + planes,)),
            ],
            compiler_params=params(4),
            name="pack",
        )(
            far(keys.reshape(peers, peer, width)),
            far(values.reshape(peers, peer, width)),
            far(queries),
            far(out_grad),
            far(doc_lengths),
            far(slot_row),
        )
    else:
        sent = [low((rows, 2 * wide))]
        kv = jnp.concatenate([keys, values], axis=1).reshape(peers, 1, peer, 2 * width)
        kv = jnp.broadcast_to(kv, kv_shape)
        pieces = [jnp.concatenate([queries, out_grad], axis=1)]
        bias = pl.pallas_call(
            functools.partial(fill_bias, peer, False),
            out_shape=jax.ShapeDtypeStruct((rows + 8, rows), jnp.float32),
            in_specs=[SMEM, VMEM],
            out_specs=VMEM,
            compiler_params=params(4),
            name="mask",
        )(doc_lengths, slot_row)
    kv = everywhere(kv)
    pieces = in_plane(pieces, pl.CostEstimate(flops=10**10, bytes_accessed=0, transcendentals=0))
    if not fine:
        kv = kv.transpose(1, 0, 2, 3).reshape(1, planes, rows, 2 * width)
    count = rows * planes
    *pieces, kv = pl.pallas_call(
        functools.partial(core_kernel, heads, len(pieces)),
        out_shape=sent + [low(kv.shape)],
        in_specs=[VMEM] * (2 + len(pieces)),
        out_specs=[VMEM] * len(sent) + [HBM],
        scratch_shapes=[
            pltpu.VMEM((count, width), jnp.bfloat16),
            pltpu.VMEM((count, width), jnp.bfloat16),
            pltpu.VMEM((rows * heads, width), jnp.bfloat16),
            pltpu.VMEM((rows * heads, width), jnp.bfloat16),
            pltpu.VMEM((count, rows * heads), jnp.bfloat16),
            pltpu.VMEM((count, rows * heads), jnp.bfloat16),
            pltpu.VMEM(kv.shape, jnp.bfloat16),
            pltpu.SemaphoreType.DMA,
        ],
        compiler_params=params(16 if planes <= 4 else 48),
        name="core",
    )(bias, kv, *pieces)
    if not fine:
        kv = kv.reshape(planes, peers, peer, 2 * width).transpose(1, 0, 2, 3)
    kv = everywhere(kv)
    if not fine:
        kv = kv.transpose(1, 0, 2, 3).reshape(1, planes, rows, 2 * width)
    pieces = in_plane(pieces)
    count = 8 * 2 if swapped else 2
    return tuple(
        pl.pallas_call(
            last_kernel,
            out_shape=[low((rows, wide))] * 2 + [low((rows, width))] * 2,
            in_specs=[VMEM] * (1 + len(pieces)),
            out_specs=[HBM] * 4,
            scratch_shapes=[
                pltpu.VMEM((rows, width), jnp.bfloat16),
                pltpu.VMEM((rows, width), jnp.bfloat16),
                pltpu.SemaphoreType.DMA((count + 2,)),
            ],
            compiler_params=params(8),
            name="last",
        )(kv, *pieces)
    )


def solution(mesh):
    rows = P(("dp", "ctx"), None)
    return jax.shard_map(
        local,
        mesh=mesh,
        in_specs=(rows, rows, rows, rows, P("dp", None), P(("dp", "ctx"))),
        out_specs=(rows, rows, rows, rows),
        check_vma=False,
    )
```

```python
import functools
import math

import jax
import jax.numpy as jnp
from jax import lax
from jax.experimental import pallas as pl
from jax.experimental.pallas import tpu as pltpu
from jax.sharding import PartitionSpec as P

HIDDEN = -1e30
ORDER_IN = (0, 3, 14, 11, 6, 18, 25, 9, 8, 2, 16, 1, 12, 27, 28, 20, 10, 15, 19, 21, 23, 7, 22, 17, 4, 24, 26, 13, 31, 29, 30, 5)
ORDER_OUT = (0, 3, 14, 11, 6, 18, 25, 9, 8, 2, 10, 1, 12, 27, 28, 20, 16, 19, 15, 21, 23, 7, 22, 17, 4, 24, 26, 13, 31, 29, 30, 5)
VMEM = pl.BlockSpec(memory_space=pltpu.VMEM)
SMEM = pl.BlockSpec(memory_space=pltpu.SMEM)
HBM = pl.BlockSpec(memory_space=pltpu.HBM)


def contract(left, right):
    return lax.dot_general(
        left, right, (((1,), (1,)), ((), ())), preferred_element_type=jnp.float32
    )


def multiply(left, right):
    return jnp.dot(left, right, preferred_element_type=jnp.float32)


def params(mib):
    return pltpu.CompilerParams(vmem_limit_bytes=mib * 1024 * 1024)


def low(shape):
    return jax.ShapeDtypeStruct(shape, jnp.bfloat16)


def near(shape):
    return pltpu.VMEM(shape, jnp.bfloat16)


def far(x):
    return pltpu.with_memory_space_constraint(x, pltpu.HBM)


def parted(blocks):
    if len(blocks) == 1:
        return [blocks[0]]
    kept, crossed = blocks
    return [half.at[k] for k in range(kept.shape[0]) for half in (kept, crossed)]


def paired(blocks):
    if len(blocks) == 1:
        return [blocks[0]]
    kept, swapped, *chips = blocks
    return [kept.at[0], swapped.at[0]] + [chip.at[core] for chip in chips for core in range(2)]


def fill_bias(peer, swapped, lengths, slot_row, bias):
    rows = slot_row.shape[1]
    own, first = lax.axis_index("dp"), lax.axis_index("ctx") * rows
    slot = jnp.broadcast_to(slot_row[...], (rows, rows))
    along = lax.broadcasted_iota(jnp.int32, (rows, rows), 1)
    down = lax.broadcasted_iota(jnp.int32, (rows, rows), 0)
    key_pos = jnp.sum(jnp.where(slot == down, along, 0), axis=1, keepdims=True)
    slot_down = slot.astype(jnp.float32).T.astype(jnp.int32)
    wanted = lax.bitwise_xor(along // peer, own) * peer + along % peer if swapped else along
    query_pos = jnp.sum(jnp.where(slot_down == wanted, down, 0), axis=0, keepdims=True)

    def later(k, carry):
        end, start = carry
        end = end + lengths[0, k]
        return end, jnp.where(query_pos + first >= end, end, start)

    _, doc_start = lax.fori_loop(
        0, lengths.shape[1], later, (jnp.int32(0), jnp.zeros((1, rows), jnp.int32))
    )
    seen = (key_pos <= query_pos) & (key_pos + first >= doc_start)
    bias[:rows, :] = jnp.where(seen, 0.0, HIDDEN)
    joined = jnp.where(first < lengths[0, 0], 0.0, HIDDEN).astype(jnp.float32)
    bias[rows:, :] = jnp.full((bias.shape[0] - rows, rows), joined)


def pack_kernel(spots, keys, values, queries, out_grad, lengths, slot_row, *refs):
    kept, crossed, bias, kv, kv_buf, block_buf, query_buf, grad_buf, length_buf, slot_buf, sems = refs
    own = lax.axis_index("dp")
    wide, width = queries.shape[1], keys.shape[2]
    peers, planes, peer = len(spots), len(spots[0]), kv.shape[1]
    come = [
        pltpu.make_async_copy(keys, kv_buf.at[:, :, :width], sems.at[0]),
        pltpu.make_async_copy(values, kv_buf.at[:, :, width:], sems.at[1]),
        pltpu.make_async_copy(queries, query_buf, sems.at[2]),
        pltpu.make_async_copy(out_grad, grad_buf, sems.at[3]),
        pltpu.make_async_copy(lengths, length_buf, sems.at[4]),
        pltpu.make_async_copy(slot_row, slot_buf, sems.at[5]),
    ]
    for copy in come:
        copy.start()
    come[0].wait()
    come[1].wait()
    for d in range(peers):
        block = kv_buf[d]
        for j in range(planes):
            block_buf[spots[d][j]] = block
    leave = pltpu.make_async_copy(block_buf, kv, sems.at[6])
    leave.start()
    come[4].wait()
    come[5].wait()
    fill_bias(peer, True, length_buf, slot_buf, bias)
    for k, buf in enumerate((query_buf, grad_buf)):
        come[2 + k].wait()
        for index, piece in enumerate(parted((kept, crossed))):
            start = pl.multiple_of(lax.bitwise_xor(own, index) * peer, peer)
            piece[:, k * wide : (k + 1) * wide] = buf[pl.ds(start, peer), :]
    leave.wait()


def pair_kernel(kept, swapped, *out):
    for k, block in enumerate(out):
        block[0] = kept[k + 1]
        block[1] = swapped[k + 1]


def core_kernel(heads, taken, spots, bias, kv, *refs):
    planes, plane = len(spots[0][0]), lax.axis_index("ctx")
    if planes > 4:
        core(heads, taken, spots, None, bias, kv, *refs)
        return
    for k in range(planes):
        pl.when(plane == k)(functools.partial(core, heads, taken, spots, k, bias, kv, *refs))


def core(heads, taken, spots, plane, bias, kv, *refs):
    pieces = paired(refs[:taken])
    *returned, kv_grad, key_all, value_all, query_flat, grad_flat, probs_all, score_all = refs[
        taken:-2
    ]
    grad_buf, sem = refs[-2:]
    returned = parted(returned)
    spots_in, spots_out = spots
    peers, planes = len(spots_in), len(spots_in[0])
    _, peer, both = kv.shape
    width = both // 2
    rows = peers * peer
    wide = heads * width
    scale = width**-0.5
    seen, before = bias[:rows, :], bias[rows : rows + 1, :]
    added = []
    for j in range(planes if plane is None else plane + 1):
        if plane is None:
            other = jnp.where(lax.axis_index("ctx") > j, before, HIDDEN)
            added.append(jnp.where(lax.axis_index("ctx") == j, seen, other))
        else:
            added.append(seen if j == plane else jnp.broadcast_to(before, (rows, rows)))
        for d in range(peers):
            at = j * rows + d * peer
            key_all[at : at + peer, :] = kv[spots_in[d][j], :, :width]
            value_all[at : at + peer, :] = kv[spots_in[d][j], :, width:]
    count = len(added) * rows
    added = jnp.concatenate(added, axis=0)
    size = pieces[0].shape[0]
    for index, piece in enumerate(pieces):
        for h in range(heads):
            at = h * rows + index * size
            query_flat[at : at + size, :] = piece[:, h * width : (h + 1) * width]
            grad_flat[at : at + size, :] = piece[:, wide + h * width : wide + (h + 1) * width]
    at_once = 2 if heads % 2 == 0 else 1
    added = jnp.concatenate([added] * at_once, axis=1)
    for h in range(0, heads, at_once):
        own = slice(h * rows, (h + at_once) * rows)
        score = contract(key_all[:count], query_flat[own, :]) * (scale * math.log2(math.e)) + added
        weight = jnp.exp2(score - jnp.max(score, axis=0, keepdims=True))
        probs = weight * (1.0 / jnp.sum(weight, axis=0, keepdims=True))
        prob_grad = contract(value_all[:count], grad_flat[own, :])
        delta = jnp.sum(probs * prob_grad, axis=0, keepdims=True)
        probs_all[:count, own] = probs.astype(jnp.bfloat16)
        score_all[:count, own] = (probs * (prob_grad - delta)).astype(jnp.bfloat16)
    key_grad = (multiply(score_all[:count], query_flat[...]) * scale).astype(jnp.bfloat16)
    value_grad = multiply(probs_all[:count], grad_flat[...]).astype(jnp.bfloat16)
    for j in range(planes):
        for d in range(peers):
            if j * rows < count:
                part = slice(j * rows + d * peer, j * rows + (d + 1) * peer)
                grad_buf[spots_out[d][j], :, :width] = key_grad[part]
                grad_buf[spots_out[d][j], :, width:] = value_grad[part]
            else:
                grad_buf[spots_out[d][j]] = jnp.zeros((peer, both), jnp.bfloat16)
    leave = pltpu.make_async_copy(grad_buf, kv_grad, sem)
    leave.start()
    attended = multiply(value_all[:count].T, probs_all[:count]).astype(jnp.bfloat16)
    query_grad = (multiply(key_all[:count].T, score_all[:count]) * scale).astype(jnp.bfloat16)
    for k, source in enumerate((attended, query_grad)):
        for h in range(heads):
            turned = source[:, h * rows : (h + 1) * rows].T
            at = (k * heads + h) * width
            for index, piece in enumerate(returned):
                piece[:, at : at + width] = turned[index * size : (index + 1) * size]
    leave.wait()


def last_kernel(spots, kv, *refs):
    *blocks, attended, query_grad, key_grad, value_grad, key_buf, value_buf, sems = refs
    pieces = paired(blocks)
    wide, size = attended.shape[1], pieces[0].shape[0]
    own = lax.axis_index("dp") if len(pieces) > 1 else 0
    copies = []
    for index, piece in enumerate(pieces):
        start = pl.multiple_of(lax.bitwise_xor(own, index) * size, size)
        for k, target in enumerate((attended, query_grad)):
            copies.append(
                pltpu.make_async_copy(
                    piece.at[:, k * wide : (k + 1) * wide],
                    target.at[pl.ds(start, size), :],
                    sems.at[len(copies)],
                )
            )
            copies[-1].start()
    _, peer, both = kv.shape
    width = both // 2
    for k, (buf, target) in enumerate(((key_buf, key_grad), (value_buf, value_grad))):
        part = slice(k * width, (k + 1) * width)
        for d, spot in enumerate(spots):
            total = kv[spot[0], :, part].astype(jnp.float32)
            for block in spot[1:]:
                total = total + kv[block, :, part].astype(jnp.float32)
            buf[d * peer : (d + 1) * peer, :] = total.astype(jnp.bfloat16)
        copies.append(pltpu.make_async_copy(buf, target, sems.at[len(copies)]))
        copies[-1].start()
    for copy in copies:
        copy.wait()


def spots_of(order, peers, planes):
    if len(order) != peers * planes:
        order = range(peers * planes)
    at = {index: spot for spot, index in enumerate(order)}
    return tuple(tuple(at[d * planes + j] for j in range(planes)) for d in range(peers))


def local(queries, keys, values, out_grad, doc_lengths, source_slot):
    rows, wide = queries.shape
    width = keys.shape[1]
    heads = wide // width
    peers, planes = lax.axis_size("dp"), lax.axis_size("ctx")
    peer = rows // peers
    fine = peer % 16 == 0
    swapped = peers == 8 and fine
    kv_shape = (peers * planes, peer, 2 * width)
    if fine:
        spots_in, spots_out = (spots_of(order, peers, planes) for order in (ORDER_IN, ORDER_OUT))
    else:
        spots_in = spots_out = (tuple(range(planes)),)

    def everywhere(x, order):
        groups = [list(order)] if len(order) == peers * planes else None
        return lax.all_to_all(
            x, ("dp", "ctx"), split_axis=0, concat_axis=0, tiled=True, axis_index_groups=groups
        )

    def by_plane(x):
        x = x.reshape(peers, planes, peer, 2 * width)
        return x.transpose(1, 0, 2, 3).reshape(planes, rows, 2 * width)

    def swap(x, mask):
        return lax.ppermute(x, "dp", [(i, i ^ mask) for i in range(peers)])

    def in_plane(pieces, cost=None):
        if not swapped:
            return [lax.all_to_all(pieces[0], "dp", split_axis=0, concat_axis=0, tiled=True)]
        kept, crossed = pieces
        crossed = swap(crossed, 1)
        chips = pl.pallas_call(
            pair_kernel,
            out_shape=[near((2, peer, 2 * wide))] * (peers // 2 - 1),
            in_specs=[VMEM] * 2,
            out_specs=[VMEM] * (peers // 2 - 1),
            compiler_params=params(4),
            cost_estimate=cost,
            name="pair",
        )(kept, crossed)
        return [kept, crossed] + [swap(chip, 2 * s + 2) for s, chip in enumerate(chips)]

    slot_row = source_slot.reshape(1, rows)
    if swapped:
        sent = [near((peers // 2, peer, 2 * wide))] * 2
        *pieces, bias, kv = pl.pallas_call(
            functools.partial(pack_kernel, spots_in),
            out_shape=sent + [pltpu.VMEM((rows + 8, rows), jnp.float32), low(kv_shape)],
            in_specs=[HBM] * 6,
            out_specs=[VMEM] * 3 + [HBM],
            scratch_shapes=[
                pltpu.VMEM((peers, peer, 2 * width), jnp.bfloat16),
                pltpu.VMEM(kv_shape, jnp.bfloat16),
                pltpu.VMEM((rows, wide), jnp.bfloat16),
                pltpu.VMEM((rows, wide), jnp.bfloat16),
                pltpu.SMEM(doc_lengths.shape, jnp.int32),
                pltpu.VMEM(slot_row.shape, jnp.int32),
                pltpu.SemaphoreType.DMA((7,)),
            ],
            compiler_params=params(4),
            name="pack",
        )(
            far(keys.reshape(peers, peer, width)),
            far(values.reshape(peers, peer, width)),
            far(queries),
            far(out_grad),
            far(doc_lengths),
            far(slot_row),
        )
    else:
        sent = [low((rows, 2 * wide))]
        kv = jnp.concatenate([keys, values], axis=1).reshape(peers, 1, peer, 2 * width)
        kv = jnp.broadcast_to(kv, (peers, planes, peer, 2 * width)).reshape(kv_shape)
        if fine:
            order = ORDER_IN if len(ORDER_IN) == peers * planes else range(peers * planes)
            kv = kv[jnp.array(order, jnp.int32)]
        pieces = [jnp.concatenate([queries, out_grad], axis=1)]
        bias = pl.pallas_call(
            functools.partial(fill_bias, peer, False),
            out_shape=jax.ShapeDtypeStruct((rows + 8, rows), jnp.float32),
            in_specs=[SMEM, VMEM],
            out_specs=VMEM,
            compiler_params=params(4),
            name="mask",
        )(doc_lengths, slot_row)
    kv = everywhere(kv, ORDER_IN)
    pieces = in_plane(pieces, pl.CostEstimate(flops=10**10, bytes_accessed=0, transcendentals=0))
    if not fine:
        kv = by_plane(kv)
    count = rows * planes
    *pieces, kv = pl.pallas_call(
        functools.partial(core_kernel, heads, len(pieces), (spots_in, spots_out)),
        out_shape=sent + [low(kv.shape)],
        in_specs=[VMEM] * (2 + len(pieces)),
        out_specs=[VMEM] * len(sent) + [HBM],
        scratch_shapes=[
            pltpu.VMEM((count, width), jnp.bfloat16),
            pltpu.VMEM((count, width), jnp.bfloat16),
            pltpu.VMEM((rows * heads, width), jnp.bfloat16),
            pltpu.VMEM((rows * heads, width), jnp.bfloat16),
            pltpu.VMEM((count, rows * heads), jnp.bfloat16),
            pltpu.VMEM((count, rows * heads), jnp.bfloat16),
            pltpu.VMEM(kv.shape, jnp.bfloat16),
            pltpu.SemaphoreType.DMA,
        ],
        compiler_params=params(16 if planes <= 4 else 48),
        name="core",
    )(bias, kv, *pieces)
    if not fine:
        kv = kv.reshape(planes, peers, peer, 2 * width).transpose(1, 0, 2, 3).reshape(kv_shape)
    kv = everywhere(kv, ORDER_OUT)
    if not fine:
        kv = by_plane(kv)
    pieces = in_plane(pieces, pl.CostEstimate(flops=10**10, bytes_accessed=0, transcendentals=0))
    count = 8 * 2 if swapped else 2
    return tuple(
        pl.pallas_call(
            functools.partial(last_kernel, spots_out),
            out_shape=[low((rows, wide))] * 2 + [low((rows, width))] * 2,
            in_specs=[VMEM] * (1 + len(pieces)),
            out_specs=[HBM] * 4,
            scratch_shapes=[
                pltpu.VMEM((rows, width), jnp.bfloat16),
                pltpu.VMEM((rows, width), jnp.bfloat16),
                pltpu.SemaphoreType.DMA((count + 2,)),
            ],
            compiler_params=params(8),
            name="last",
        )(kv, *pieces)
    )


def solution(mesh):
    rows = P(("dp", "ctx"), None)
    return jax.shard_map(
        local,
        mesh=mesh,
        in_specs=(rows, rows, rows, rows, P("dp", None), P(("dp", "ctx"))),
        out_specs=(rows, rows, rows, rows),
        check_vma=False,
    )
```

```python
import functools
import math

import jax
import jax.numpy as jnp
from jax import lax
from jax.experimental import pallas as pl
from jax.experimental.pallas import tpu as pltpu
from jax.sharding import PartitionSpec as P

HIDDEN = -1e30
ORDER_IN = (0, 3, 14, 11, 6, 18, 25, 9, 8, 2, 16, 1, 12, 27, 28, 20, 10, 15, 19, 21, 23, 7, 22, 17, 4, 24, 26, 13, 31, 29, 30, 5)
ORDER_OUT = (0, 3, 14, 11, 6, 18, 25, 9, 8, 2, 10, 1, 12, 27, 28, 20, 16, 19, 15, 21, 23, 7, 22, 17, 4, 24, 26, 13, 31, 29, 30, 5)
CHIPS = (0, 3, 2, 1)
MASKS = tuple(2 * chip + core for chip in CHIPS for core in range(2))
VMEM = pl.BlockSpec(memory_space=pltpu.VMEM)
SMEM = pl.BlockSpec(memory_space=pltpu.SMEM)
HBM = pl.BlockSpec(memory_space=pltpu.HBM)


def contract(left, right):
    return lax.dot_general(
        left, right, (((1,), (1,)), ((), ())), preferred_element_type=jnp.float32
    )


def multiply(left, right):
    return jnp.dot(left, right, preferred_element_type=jnp.float32)


def params(mib):
    return pltpu.CompilerParams(vmem_limit_bytes=mib * 1024 * 1024)


def low(shape):
    return jax.ShapeDtypeStruct(shape, jnp.bfloat16)


def near(shape):
    return pltpu.VMEM(shape, jnp.bfloat16)


def far(x):
    return pltpu.with_memory_space_constraint(x, pltpu.HBM)


def parted(blocks):
    if len(blocks) == 1:
        return [blocks[0]]
    kept, crossed = blocks
    return [half.at[k] for k in range(kept.shape[0]) for half in (kept, crossed)]


def paired(blocks):
    if len(blocks) == 1:
        return [blocks[0]]
    kept, swapped, *chips = blocks
    return [kept.at[0], swapped.at[0]] + [chip.at[core] for chip in chips for core in range(2)]


def fill_bias(peer, swapped, lengths, slot_row, bias):
    rows = slot_row.shape[1]
    own, first = lax.axis_index("dp"), lax.axis_index("ctx") * rows
    slot = jnp.broadcast_to(slot_row[...], (rows, rows))
    along = lax.broadcasted_iota(jnp.int32, (rows, rows), 1)
    down = lax.broadcasted_iota(jnp.int32, (rows, rows), 0)
    key_pos = jnp.sum(jnp.where(slot == down, along, 0), axis=1, keepdims=True)
    slot_down = slot.astype(jnp.float32).T.astype(jnp.int32)
    if swapped:
        mask = jnp.zeros_like(along)
        for index, value in enumerate(MASKS):
            mask = jnp.where(along // peer == index, value, mask)
        wanted = lax.bitwise_xor(mask, own) * peer + along % peer
    else:
        wanted = along
    query_pos = jnp.sum(jnp.where(slot_down == wanted, down, 0), axis=0, keepdims=True)

    def later(k, carry):
        end, start = carry
        end = end + lengths[0, k]
        return end, jnp.where(query_pos + first >= end, end, start)

    _, doc_start = lax.fori_loop(
        0, lengths.shape[1], later, (jnp.int32(0), jnp.zeros((1, rows), jnp.int32))
    )
    seen = (key_pos <= query_pos) & (key_pos + first >= doc_start)
    bias[:rows, :] = jnp.where(seen, 0.0, HIDDEN)
    joined = jnp.where(first < lengths[0, 0], 0.0, HIDDEN).astype(jnp.float32)
    bias[rows:, :] = jnp.full((bias.shape[0] - rows, rows), joined)


def pack_kernel(spots, keys, values, queries, out_grad, lengths, slot_row, *refs):
    kept, crossed, bias, kv, kv_buf, block_buf, query_buf, grad_buf, length_buf, slot_buf, sems = refs
    own = lax.axis_index("dp")
    wide, width = queries.shape[1], keys.shape[2]
    peers, planes, peer = len(spots), len(spots[0]), kv.shape[1]
    come = [
        pltpu.make_async_copy(keys, kv_buf.at[:, :, :width], sems.at[0]),
        pltpu.make_async_copy(values, kv_buf.at[:, :, width:], sems.at[1]),
        pltpu.make_async_copy(queries, query_buf, sems.at[2]),
        pltpu.make_async_copy(out_grad, grad_buf, sems.at[3]),
        pltpu.make_async_copy(lengths, length_buf, sems.at[4]),
        pltpu.make_async_copy(slot_row, slot_buf, sems.at[5]),
    ]
    for copy in come:
        copy.start()
    come[0].wait()
    come[1].wait()
    for d in range(peers):
        block = kv_buf[d]
        for j in range(planes):
            block_buf[spots[d][j]] = block
    leave = pltpu.make_async_copy(block_buf, kv, sems.at[6])
    leave.start()
    come[4].wait()
    come[5].wait()
    fill_bias(peer, True, length_buf, slot_buf, bias)
    for k, buf in enumerate((query_buf, grad_buf)):
        come[2 + k].wait()
        for index, piece in enumerate(parted((kept, crossed))):
            start = pl.multiple_of(lax.bitwise_xor(own, MASKS[index]) * peer, peer)
            piece[:, k * wide : (k + 1) * wide] = buf[pl.ds(start, peer), :]
    leave.wait()


def pair_kernel(kept, swapped, *out):
    for k, block in enumerate(out):
        block[0] = kept[k + 1]
        block[1] = swapped[k + 1]


def core_kernel(heads, taken, spots, bias, kv, *refs):
    planes, plane = len(spots[0][0]), lax.axis_index("ctx")
    if planes > 4:
        core(heads, taken, spots, None, bias, kv, *refs)
        return
    for k in range(planes):
        pl.when(plane == k)(functools.partial(core, heads, taken, spots, k, bias, kv, *refs))


def core(heads, taken, spots, plane, bias, kv, *refs):
    pieces = paired(refs[:taken])
    *returned, kv_grad, key_all, value_all, query_flat, grad_flat, probs_all, score_all = refs[
        taken:-2
    ]
    grad_buf, sem = refs[-2:]
    returned = parted(returned)
    spots_in, spots_out = spots
    peers, planes = len(spots_in), len(spots_in[0])
    _, peer, both = kv.shape
    width = both // 2
    rows = peers * peer
    wide = heads * width
    scale = width**-0.5
    seen, before = bias[:rows, :], bias[rows : rows + 1, :]
    added = []
    for j in range(planes if plane is None else plane + 1):
        if plane is None:
            other = jnp.where(lax.axis_index("ctx") > j, before, HIDDEN)
            added.append(jnp.where(lax.axis_index("ctx") == j, seen, other))
        else:
            added.append(seen if j == plane else jnp.broadcast_to(before, (rows, rows)))
        for d in range(peers):
            at = j * rows + d * peer
            key_all[at : at + peer, :] = kv[spots_in[d][j], :, :width]
            value_all[at : at + peer, :] = kv[spots_in[d][j], :, width:]
    count = len(added) * rows
    added = jnp.concatenate(added, axis=0)
    size = pieces[0].shape[0]
    for index, piece in enumerate(pieces):
        for h in range(heads):
            at = h * rows + index * size
            query_flat[at : at + size, :] = piece[:, h * width : (h + 1) * width]
            grad_flat[at : at + size, :] = piece[:, wide + h * width : wide + (h + 1) * width]
    at_once = 2 if heads % 2 == 0 else 1
    added = jnp.concatenate([added] * at_once, axis=1)
    for h in range(0, heads, at_once):
        own = slice(h * rows, (h + at_once) * rows)
        score = contract(key_all[:count], query_flat[own, :]) * (scale * math.log2(math.e)) + added
        weight = jnp.exp2(score - jnp.max(score, axis=0, keepdims=True))
        probs = weight * (1.0 / jnp.sum(weight, axis=0, keepdims=True))
        prob_grad = contract(value_all[:count], grad_flat[own, :])
        delta = jnp.sum(probs * prob_grad, axis=0, keepdims=True)
        probs_all[:count, own] = probs.astype(jnp.bfloat16)
        score_all[:count, own] = (probs * (prob_grad - delta)).astype(jnp.bfloat16)
    key_grad = (multiply(score_all[:count], query_flat[...]) * scale).astype(jnp.bfloat16)
    value_grad = multiply(probs_all[:count], grad_flat[...]).astype(jnp.bfloat16)
    for j in range(planes):
        for d in range(peers):
            if j * rows < count:
                part = slice(j * rows + d * peer, j * rows + (d + 1) * peer)
                grad_buf[spots_out[d][j], :, :width] = key_grad[part]
                grad_buf[spots_out[d][j], :, width:] = value_grad[part]
            else:
                grad_buf[spots_out[d][j]] = jnp.zeros((peer, both), jnp.bfloat16)
    leave = pltpu.make_async_copy(grad_buf, kv_grad, sem)
    leave.start()
    attended = multiply(value_all[:count].T, probs_all[:count]).astype(jnp.bfloat16)
    query_grad = (multiply(key_all[:count].T, score_all[:count]) * scale).astype(jnp.bfloat16)
    for k, source in enumerate((attended, query_grad)):
        for h in range(heads):
            turned = source[:, h * rows : (h + 1) * rows].T
            at = (k * heads + h) * width
            for index, piece in enumerate(returned):
                piece[:, at : at + width] = turned[index * size : (index + 1) * size]
    leave.wait()


def last_kernel(spots, kv, *refs):
    *blocks, attended, query_grad, key_grad, value_grad, key_buf, value_buf, sems = refs
    pieces = paired(blocks)
    wide, size = attended.shape[1], pieces[0].shape[0]
    own = lax.axis_index("dp") if len(pieces) > 1 else None
    copies = []
    for index, piece in enumerate(pieces):
        start = pl.multiple_of(lax.bitwise_xor(own, MASKS[index]) * size, size) if own is not None else 0
        for k, target in enumerate((attended, query_grad)):
            copies.append(
                pltpu.make_async_copy(
                    piece.at[:, k * wide : (k + 1) * wide],
                    target.at[pl.ds(start, size), :],
                    sems.at[len(copies)],
                )
            )
            copies[-1].start()
    _, peer, both = kv.shape
    width = both // 2
    for k, (buf, target) in enumerate(((key_buf, key_grad), (value_buf, value_grad))):
        part = slice(k * width, (k + 1) * width)
        for d, spot in enumerate(spots):
            total = kv[spot[0], :, part].astype(jnp.float32)
            for block in spot[1:]:
                total = total + kv[block, :, part].astype(jnp.float32)
            buf[d * peer : (d + 1) * peer, :] = total.astype(jnp.bfloat16)
        copies.append(pltpu.make_async_copy(buf, target, sems.at[len(copies)]))
        copies[-1].start()
    for copy in copies:
        copy.wait()


def spots_of(order, peers, planes):
    at = {index: spot for spot, index in enumerate(order or range(peers * planes))}
    return tuple(tuple(at[d * planes + j] for j in range(planes)) for d in range(peers))


def local(queries, keys, values, out_grad, doc_lengths, source_slot):
    rows, wide = queries.shape
    width = keys.shape[1]
    heads = wide // width
    peers, planes = lax.axis_size("dp"), lax.axis_size("ctx")
    peer = rows // peers
    fine = peer % 16 == 0
    swapped = peers == 8 and fine
    kv_shape = (peers * planes, peer, 2 * width)
    measured = swapped and planes == 4
    order_in, order_out = (ORDER_IN, ORDER_OUT) if measured else (None, None)
    if fine:
        spots_in, spots_out = (spots_of(order, peers, planes) for order in (order_in, order_out))
    else:
        spots_in = spots_out = (tuple(range(planes)),)

    def everywhere(x, order):
        groups = [list(order)] if order else None
        return lax.all_to_all(
            x, ("dp", "ctx"), split_axis=0, concat_axis=0, tiled=True, axis_index_groups=groups
        )

    def by_plane(x):
        x = x.reshape(peers, planes, peer, 2 * width)
        return x.transpose(1, 0, 2, 3).reshape(planes, rows, 2 * width)

    def swap(x, mask):
        return lax.ppermute(x, "dp", [(i, i ^ mask) for i in range(peers)])

    def in_plane(pieces, cost=None):
        if not swapped:
            return [lax.all_to_all(pieces[0], "dp", split_axis=0, concat_axis=0, tiled=True)]
        kept, crossed = pieces
        crossed = swap(crossed, 1)
        chips = pl.pallas_call(
            pair_kernel,
            out_shape=[near((2, peer, 2 * wide))] * (peers // 2 - 1),
            in_specs=[VMEM] * 2,
            out_specs=[VMEM] * (peers // 2 - 1),
            compiler_params=params(4),
            cost_estimate=cost,
            name="pair",
        )(kept, crossed)
        return [kept, crossed] + [swap(chip, 2 * mask) for chip, mask in zip(chips, CHIPS[1:])]

    slot_row = source_slot.reshape(1, rows)
    if swapped:
        sent = [near((peers // 2, peer, 2 * wide))] * 2
        *pieces, bias, kv = pl.pallas_call(
            functools.partial(pack_kernel, spots_in),
            out_shape=sent + [pltpu.VMEM((rows + 8, rows), jnp.float32), low(kv_shape)],
            in_specs=[HBM] * 6,
            out_specs=[VMEM] * 3 + [HBM],
            scratch_shapes=[
                pltpu.VMEM((peers, peer, 2 * width), jnp.bfloat16),
                pltpu.VMEM(kv_shape, jnp.bfloat16),
                pltpu.VMEM((rows, wide), jnp.bfloat16),
                pltpu.VMEM((rows, wide), jnp.bfloat16),
                pltpu.SMEM(doc_lengths.shape, jnp.int32),
                pltpu.VMEM(slot_row.shape, jnp.int32),
                pltpu.SemaphoreType.DMA((7,)),
            ],
            compiler_params=params(4),
            name="pack",
        )(
            far(keys.reshape(peers, peer, width)),
            far(values.reshape(peers, peer, width)),
            far(queries),
            far(out_grad),
            far(doc_lengths),
            far(slot_row),
        )
    else:
        sent = [low((rows, 2 * wide))]
        kv = jnp.concatenate([keys, values], axis=1).reshape(peers, 1, peer, 2 * width)
        kv = jnp.broadcast_to(kv, (peers, planes, peer, 2 * width)).reshape(kv_shape)
        pieces = [jnp.concatenate([queries, out_grad], axis=1)]
        bias = pl.pallas_call(
            functools.partial(fill_bias, peer, False),
            out_shape=jax.ShapeDtypeStruct((rows + 8, rows), jnp.float32),
            in_specs=[SMEM, VMEM],
            out_specs=VMEM,
            compiler_params=params(4),
            name="mask",
        )(doc_lengths, slot_row)
    kv = everywhere(kv, order_in)
    pieces = in_plane(pieces, pl.CostEstimate(flops=10**10, bytes_accessed=0, transcendentals=0))
    if not fine:
        kv = by_plane(kv)
    count = rows * planes
    *pieces, kv = pl.pallas_call(
        functools.partial(core_kernel, heads, len(pieces), (spots_in, spots_out)),
        out_shape=sent + [low(kv.shape)],
        in_specs=[VMEM] * (2 + len(pieces)),
        out_specs=[VMEM] * len(sent) + [HBM],
        scratch_shapes=[
            pltpu.VMEM((count, width), jnp.bfloat16),
            pltpu.VMEM((count, width), jnp.bfloat16),
            pltpu.VMEM((rows * heads, width), jnp.bfloat16),
            pltpu.VMEM((rows * heads, width), jnp.bfloat16),
            pltpu.VMEM((count, rows * heads), jnp.bfloat16),
            pltpu.VMEM((count, rows * heads), jnp.bfloat16),
            pltpu.VMEM(kv.shape, jnp.bfloat16),
            pltpu.SemaphoreType.DMA,
        ],
        compiler_params=params(16 if planes <= 4 else 48),
        name="core",
    )(bias, kv, *pieces)
    if not fine:
        kv = kv.reshape(planes, peers, peer, 2 * width).transpose(1, 0, 2, 3).reshape(kv_shape)
    kv = everywhere(kv, order_out)
    if not fine:
        kv = by_plane(kv)
    pieces = in_plane(pieces, pl.CostEstimate(flops=10**10, bytes_accessed=0, transcendentals=0))
    count = 8 * 2 if swapped else 2
    return tuple(
        pl.pallas_call(
            functools.partial(last_kernel, spots_out),
            out_shape=[low((rows, wide))] * 2 + [low((rows, width))] * 2,
            in_specs=[VMEM] * (1 + len(pieces)),
            out_specs=[HBM] * 4,
            scratch_shapes=[
                pltpu.VMEM((rows, width), jnp.bfloat16),
                pltpu.VMEM((rows, width), jnp.bfloat16),
                pltpu.SemaphoreType.DMA((count + 2,)),
            ],
            compiler_params=params(8),
            name="last",
        )(kv, *pieces)
    )


def solution(mesh):
    rows = P(("dp", "ctx"), None)
    return jax.shard_map(
        local,
        mesh=mesh,
        in_specs=(rows, rows, rows, rows, P("dp", None), P(("dp", "ctx"))),
        out_specs=(rows, rows, rows, rows),
        check_vma=False,
    )
```

```python
import functools
import math

import jax
import jax.numpy as jnp
from jax import lax
from jax.experimental import pallas as pl
from jax.experimental.pallas import tpu as pltpu
from jax.sharding import PartitionSpec as P

HIDDEN = -1e30
ORDER_IN = (0, 3, 14, 11, 6, 18, 25, 9, 8, 2, 16, 1, 12, 27, 28, 20, 10, 15, 19, 21, 23, 7, 22, 17, 4, 24, 26, 13, 31, 29, 30, 5)
ORDER_OUT = (0, 3, 14, 11, 6, 18, 25, 9, 8, 2, 10, 1, 12, 27, 28, 20, 16, 19, 15, 21, 23, 7, 22, 17, 4, 24, 26, 13, 31, 29, 30, 5)
CHIPS = (0, 3, 2, 1)
CHIPS_BACK = (0, 3, 1, 2)
MASKS, MASKS_BACK = (
    tuple(2 * chip + core for chip in chips for core in range(2)) for chips in (CHIPS, CHIPS_BACK)
)
VMEM = pl.BlockSpec(memory_space=pltpu.VMEM)
SMEM = pl.BlockSpec(memory_space=pltpu.SMEM)
HBM = pl.BlockSpec(memory_space=pltpu.HBM)


def contract(left, right):
    return lax.dot_general(
        left, right, (((1,), (1,)), ((), ())), preferred_element_type=jnp.float32
    )


def multiply(left, right):
    return jnp.dot(left, right, preferred_element_type=jnp.float32)


def params(mib):
    return pltpu.CompilerParams(vmem_limit_bytes=mib * 1024 * 1024)


def low(shape):
    return jax.ShapeDtypeStruct(shape, jnp.bfloat16)


def near(shape):
    return pltpu.VMEM(shape, jnp.bfloat16)


def far(x):
    return pltpu.with_memory_space_constraint(x, pltpu.HBM)


def parted(blocks):
    if len(blocks) == 1:
        return [blocks[0]]
    kept, crossed = blocks
    return [half.at[k] for k in range(kept.shape[0]) for half in (kept, crossed)]


def paired(blocks):
    if len(blocks) == 1:
        return [blocks[0]]
    kept, swapped, *chips = blocks
    return [kept.at[0], swapped.at[0]] + [chip.at[core] for chip in chips for core in range(2)]


def fill_bias(peer, swapped, lengths, slot_row, bias):
    rows = slot_row.shape[1]
    own, first = lax.axis_index("dp"), lax.axis_index("ctx") * rows
    slot = jnp.broadcast_to(slot_row[...], (rows, rows))
    along = lax.broadcasted_iota(jnp.int32, (rows, rows), 1)
    down = lax.broadcasted_iota(jnp.int32, (rows, rows), 0)
    key_pos = jnp.sum(jnp.where(slot == down, along, 0), axis=1, keepdims=True)
    slot_down = slot.astype(jnp.float32).T.astype(jnp.int32)
    if swapped:
        mask = jnp.zeros_like(along)
        for index, value in enumerate(MASKS):
            mask = jnp.where(along // peer == index, value, mask)
        wanted = lax.bitwise_xor(mask, own) * peer + along % peer
    else:
        wanted = along
    query_pos = jnp.sum(jnp.where(slot_down == wanted, down, 0), axis=0, keepdims=True)

    def later(k, carry):
        end, start = carry
        end = end + lengths[0, k]
        return end, jnp.where(query_pos + first >= end, end, start)

    _, doc_start = lax.fori_loop(
        0, lengths.shape[1], later, (jnp.int32(0), jnp.zeros((1, rows), jnp.int32))
    )
    seen = (key_pos <= query_pos) & (key_pos + first >= doc_start)
    bias[:rows, :] = jnp.where(seen, 0.0, HIDDEN)
    joined = jnp.where(first < lengths[0, 0], 0.0, HIDDEN).astype(jnp.float32)
    bias[rows:, :] = jnp.full((bias.shape[0] - rows, rows), joined)


def pack_kernel(spots, keys, values, queries, out_grad, lengths, slot_row, *refs):
    kept, crossed, bias, kv, kv_buf, block_buf, query_buf, grad_buf, length_buf, slot_buf, sems = refs
    own = lax.axis_index("dp")
    wide, width = queries.shape[1], keys.shape[2]
    peers, planes, peer = len(spots), len(spots[0]), kv.shape[1]
    come = [
        pltpu.make_async_copy(keys, kv_buf.at[:, :, :width], sems.at[0]),
        pltpu.make_async_copy(values, kv_buf.at[:, :, width:], sems.at[1]),
        pltpu.make_async_copy(queries, query_buf, sems.at[2]),
        pltpu.make_async_copy(out_grad, grad_buf, sems.at[3]),
        pltpu.make_async_copy(lengths, length_buf, sems.at[4]),
        pltpu.make_async_copy(slot_row, slot_buf, sems.at[5]),
    ]
    for copy in come:
        copy.start()
    come[0].wait()
    come[1].wait()
    for d in range(peers):
        block = kv_buf[d]
        for j in range(planes):
            block_buf[spots[d][j]] = block
    leave = pltpu.make_async_copy(block_buf, kv, sems.at[6])
    leave.start()
    come[4].wait()
    come[5].wait()
    fill_bias(peer, True, length_buf, slot_buf, bias)
    for k, buf in enumerate((query_buf, grad_buf)):
        come[2 + k].wait()
        for index, piece in enumerate(parted((kept, crossed))):
            start = pl.multiple_of(lax.bitwise_xor(own, MASKS[index]) * peer, peer)
            piece[:, k * wide : (k + 1) * wide] = buf[pl.ds(start, peer), :]
    leave.wait()


def pair_kernel(kept, swapped, *out):
    for k, block in enumerate(out):
        block[0] = kept[k + 1]
        block[1] = swapped[k + 1]


def core_kernel(heads, taken, spots, bias, kv, *refs):
    planes, plane = len(spots[0][0]), lax.axis_index("ctx")
    if planes > 4:
        core(heads, taken, spots, None, bias, kv, *refs)
        return
    for k in range(planes):
        pl.when(plane == k)(functools.partial(core, heads, taken, spots, k, bias, kv, *refs))


def core(heads, taken, spots, plane, bias, kv, *refs):
    pieces = paired(refs[:taken])
    *returned, kv_grad, key_all, value_all, query_flat, grad_flat, probs_all, score_all = refs[
        taken:-2
    ]
    grad_buf, sem = refs[-2:]
    returned = parted(returned)
    spots_in, spots_out = spots
    peers, planes = len(spots_in), len(spots_in[0])
    _, peer, both = kv.shape
    width = both // 2
    rows = peers * peer
    wide = heads * width
    scale = width**-0.5
    seen, before = bias[:rows, :], bias[rows : rows + 1, :]
    added = []
    for j in range(planes if plane is None else plane + 1):
        if plane is None:
            other = jnp.where(lax.axis_index("ctx") > j, before, HIDDEN)
            added.append(jnp.where(lax.axis_index("ctx") == j, seen, other))
        else:
            added.append(seen if j == plane else jnp.broadcast_to(before, (rows, rows)))
        for d in range(peers):
            at = j * rows + d * peer
            key_all[at : at + peer, :] = kv[spots_in[d][j], :, :width]
            value_all[at : at + peer, :] = kv[spots_in[d][j], :, width:]
    count = len(added) * rows
    added = jnp.concatenate(added, axis=0)
    size = pieces[0].shape[0]
    for index, piece in enumerate(pieces):
        for h in range(heads):
            at = h * rows + index * size
            query_flat[at : at + size, :] = piece[:, h * width : (h + 1) * width]
            grad_flat[at : at + size, :] = piece[:, wide + h * width : wide + (h + 1) * width]
    at_once = 2 if heads % 2 == 0 else 1
    added = jnp.concatenate([added] * at_once, axis=1)
    for h in range(0, heads, at_once):
        own = slice(h * rows, (h + at_once) * rows)
        score = contract(key_all[:count], query_flat[own, :]) * (scale * math.log2(math.e)) + added
        weight = jnp.exp2(score - jnp.max(score, axis=0, keepdims=True))
        probs = weight * (1.0 / jnp.sum(weight, axis=0, keepdims=True))
        prob_grad = contract(value_all[:count], grad_flat[own, :])
        delta = jnp.sum(probs * prob_grad, axis=0, keepdims=True)
        probs_all[:count, own] = probs.astype(jnp.bfloat16)
        score_all[:count, own] = (probs * (prob_grad - delta)).astype(jnp.bfloat16)
    leave = []
    for k, (left, right, factor) in enumerate(
        ((probs_all, grad_flat, None), (score_all, query_flat, scale))
    ):
        half = slice((1 - k) * width, (2 - k) * width)
        total = multiply(left[:count], right[...])
        total = (total if factor is None else total * factor).astype(jnp.bfloat16)
        for j in range(planes):
            for d in range(peers):
                at = j * rows + d * peer
                part = total[at : at + peer] if at < count else jnp.zeros((peer, width), jnp.bfloat16)
                grad_buf[spots_out[d][j], :, half] = part
        leave.append(
            pltpu.make_async_copy(grad_buf.at[:, :, half], kv_grad.at[:, :, half], sem.at[k])
        )
        leave[-1].start()
    attended = multiply(value_all[:count].T, probs_all[:count]).astype(jnp.bfloat16)
    query_grad = (multiply(key_all[:count].T, score_all[:count]) * scale).astype(jnp.bfloat16)
    for k, source in enumerate((attended, query_grad)):
        for h in range(heads):
            turned = source[:, h * rows : (h + 1) * rows].T
            at = (k * heads + h) * width
            for index, piece in enumerate(returned):
                from_row = MASKS.index(MASKS_BACK[index]) * size if len(returned) > 1 else 0
                piece[:, at : at + width] = turned[from_row : from_row + size]
    for copy in leave:
        copy.wait()


def last_kernel(spots, kv, *refs):
    *blocks, attended, query_grad, key_grad, value_grad, key_buf, value_buf, sems = refs
    pieces = paired(blocks)
    wide, size = attended.shape[1], pieces[0].shape[0]
    own = lax.axis_index("dp") if len(pieces) > 1 else None
    copies = []
    for index, piece in enumerate(pieces):
        start = pl.multiple_of(lax.bitwise_xor(own, MASKS_BACK[index]) * size, size) if own is not None else 0
        for k, target in enumerate((attended, query_grad)):
            copies.append(
                pltpu.make_async_copy(
                    piece.at[:, k * wide : (k + 1) * wide],
                    target.at[pl.ds(start, size), :],
                    sems.at[len(copies)],
                )
            )
            copies[-1].start()
    _, peer, both = kv.shape
    width = both // 2
    for k, (buf, target) in enumerate(((key_buf, key_grad), (value_buf, value_grad))):
        part = slice(k * width, (k + 1) * width)
        for d, spot in enumerate(spots):
            total = kv[spot[0], :, part].astype(jnp.float32)
            for block in spot[1:]:
                total = total + kv[block, :, part].astype(jnp.float32)
            buf[d * peer : (d + 1) * peer, :] = total.astype(jnp.bfloat16)
        copies.append(pltpu.make_async_copy(buf, target, sems.at[len(copies)]))
        copies[-1].start()
    for copy in copies:
        copy.wait()


def spots_of(order, peers, planes):
    at = {index: spot for spot, index in enumerate(order or range(peers * planes))}
    return tuple(tuple(at[d * planes + j] for j in range(planes)) for d in range(peers))


def local(queries, keys, values, out_grad, doc_lengths, source_slot):
    rows, wide = queries.shape
    width = keys.shape[1]
    heads = wide // width
    peers, planes = lax.axis_size("dp"), lax.axis_size("ctx")
    peer = rows // peers
    fine = peer % 16 == 0
    swapped = peers == 8 and fine
    kv_shape = (peers * planes, peer, 2 * width)
    measured = swapped and planes == 4
    order_in, order_out = (ORDER_IN, ORDER_OUT) if measured else (None, None)
    if fine:
        spots_in, spots_out = (spots_of(order, peers, planes) for order in (order_in, order_out))
    else:
        spots_in = spots_out = (tuple(range(planes)),)

    def everywhere(x, order):
        groups = [list(order)] if order else None
        return lax.all_to_all(
            x, ("dp", "ctx"), split_axis=0, concat_axis=0, tiled=True, axis_index_groups=groups
        )

    def by_plane(x):
        x = x.reshape(peers, planes, peer, 2 * width)
        return x.transpose(1, 0, 2, 3).reshape(planes, rows, 2 * width)

    def swap(x, mask):
        return lax.ppermute(x, "dp", [(i, i ^ mask) for i in range(peers)])

    def in_plane(pieces, order, cost):
        if not swapped:
            return [lax.all_to_all(pieces[0], "dp", split_axis=0, concat_axis=0, tiled=True)]
        kept, crossed = pieces
        crossed = swap(crossed, 1)
        chips = pl.pallas_call(
            pair_kernel,
            out_shape=[near((2, peer, 2 * wide))] * (peers // 2 - 1),
            in_specs=[VMEM] * 2,
            out_specs=[VMEM] * (peers // 2 - 1),
            compiler_params=params(4),
            cost_estimate=cost,
            name="pair",
        )(kept, crossed)
        return [kept, crossed] + [swap(chip, 2 * mask) for chip, mask in zip(chips, order[1:])]

    slot_row = source_slot.reshape(1, rows)
    if swapped:
        sent = [near((peers // 2, peer, 2 * wide))] * 2
        *pieces, bias, kv = pl.pallas_call(
            functools.partial(pack_kernel, spots_in),
            out_shape=sent + [pltpu.VMEM((rows + 8, rows), jnp.float32), low(kv_shape)],
            in_specs=[HBM] * 6,
            out_specs=[VMEM] * 3 + [HBM],
            scratch_shapes=[
                pltpu.VMEM((peers, peer, 2 * width), jnp.bfloat16),
                pltpu.VMEM(kv_shape, jnp.bfloat16),
                pltpu.VMEM((rows, wide), jnp.bfloat16),
                pltpu.VMEM((rows, wide), jnp.bfloat16),
                pltpu.SMEM(doc_lengths.shape, jnp.int32),
                pltpu.VMEM(slot_row.shape, jnp.int32),
                pltpu.SemaphoreType.DMA((7,)),
            ],
            compiler_params=params(4),
            name="pack",
        )(
            far(keys.reshape(peers, peer, width)),
            far(values.reshape(peers, peer, width)),
            far(queries),
            far(out_grad),
            far(doc_lengths),
            far(slot_row),
        )
    else:
        sent = [low((rows, 2 * wide))]
        kv = jnp.concatenate([keys, values], axis=1).reshape(peers, 1, peer, 2 * width)
        kv = jnp.broadcast_to(kv, (peers, planes, peer, 2 * width)).reshape(kv_shape)
        pieces = [jnp.concatenate([queries, out_grad], axis=1)]
        bias = pl.pallas_call(
            functools.partial(fill_bias, peer, False),
            out_shape=jax.ShapeDtypeStruct((rows + 8, rows), jnp.float32),
            in_specs=[SMEM, VMEM],
            out_specs=VMEM,
            compiler_params=params(4),
            name="mask",
        )(doc_lengths, slot_row)
    kv = everywhere(kv, order_in)
    pieces = in_plane(pieces, CHIPS, pl.CostEstimate(flops=10**10, bytes_accessed=0, transcendentals=0))
    if not fine:
        kv = by_plane(kv)
    count = rows * planes
    *pieces, kv = pl.pallas_call(
        functools.partial(core_kernel, heads, len(pieces), (spots_in, spots_out)),
        out_shape=sent + [low(kv.shape)],
        in_specs=[VMEM] * (2 + len(pieces)),
        out_specs=[VMEM] * len(sent) + [HBM],
        scratch_shapes=[
            pltpu.VMEM((count, width), jnp.bfloat16),
            pltpu.VMEM((count, width), jnp.bfloat16),
            pltpu.VMEM((rows * heads, width), jnp.bfloat16),
            pltpu.VMEM((rows * heads, width), jnp.bfloat16),
            pltpu.VMEM((count, rows * heads), jnp.bfloat16),
            pltpu.VMEM((count, rows * heads), jnp.bfloat16),
            pltpu.VMEM(kv.shape, jnp.bfloat16),
            pltpu.SemaphoreType.DMA((2,)),
        ],
        compiler_params=params(16 if planes <= 4 else 48),
        name="core",
    )(bias, kv, *pieces)
    if not fine:
        kv = kv.reshape(planes, peers, peer, 2 * width).transpose(1, 0, 2, 3).reshape(kv_shape)
    kv = everywhere(kv, order_out)
    if not fine:
        kv = by_plane(kv)
    pieces = in_plane(pieces, CHIPS_BACK, pl.CostEstimate(flops=10**10, bytes_accessed=0, transcendentals=0))
    count = 8 * 2 if swapped else 2
    return tuple(
        pl.pallas_call(
            functools.partial(last_kernel, spots_out),
            out_shape=[low((rows, wide))] * 2 + [low((rows, width))] * 2,
            in_specs=[VMEM] * (1 + len(pieces)),
            out_specs=[HBM] * 4,
            scratch_shapes=[
                pltpu.VMEM((rows, width), jnp.bfloat16),
                pltpu.VMEM((rows, width), jnp.bfloat16),
                pltpu.SemaphoreType.DMA((count + 2,)),
            ],
            compiler_params=params(8),
            name="last",
        )(kv, *pieces)
    )


def solution(mesh):
    rows = P(("dp", "ctx"), None)
    return jax.shard_map(
        local,
        mesh=mesh,
        in_specs=(rows, rows, rows, rows, P("dp", None), P(("dp", "ctx"))),
        out_specs=(rows, rows, rows, rows),
        check_vma=False,
    )
```

```python
import functools
import math

import jax
import jax.numpy as jnp
from jax import lax
from jax.experimental import pallas as pl
from jax.experimental.pallas import tpu as pltpu
from jax.sharding import PartitionSpec as P

HIDDEN = -1e30
ORDER_IN = (0, 3, 14, 11, 6, 18, 25, 9, 8, 2, 16, 1, 12, 27, 28, 20, 10, 15, 19, 21, 23, 7, 22, 17, 4, 24, 26, 13, 31, 29, 30, 5)
ORDER_OUT = (0, 3, 14, 11, 6, 18, 25, 9, 8, 2, 10, 28, 12, 27, 1, 20, 16, 19, 15, 21, 23, 7, 22, 17, 4, 24, 26, 13, 31, 29, 30, 5)
CHIPS = (0, 3, 2, 1)
CHIPS_BACK = (0, 3, 1, 2)
MASKS, MASKS_BACK = (
    tuple(2 * chip + core for chip in chips for core in range(2)) for chips in (CHIPS, CHIPS_BACK)
)
VMEM = pl.BlockSpec(memory_space=pltpu.VMEM)
SMEM = pl.BlockSpec(memory_space=pltpu.SMEM)
HBM = pl.BlockSpec(memory_space=pltpu.HBM)


def contract(left, right):
    return lax.dot_general(
        left, right, (((1,), (1,)), ((), ())), preferred_element_type=jnp.float32
    )


def multiply(left, right):
    return jnp.dot(left, right, preferred_element_type=jnp.float32)


def params(mib):
    return pltpu.CompilerParams(vmem_limit_bytes=mib * 1024 * 1024)


def low(shape):
    return jax.ShapeDtypeStruct(shape, jnp.bfloat16)


def near(shape):
    return pltpu.VMEM(shape, jnp.bfloat16)


def far(x):
    return pltpu.with_memory_space_constraint(x, pltpu.HBM)


def parted(blocks):
    if len(blocks) == 1:
        return [blocks[0]]
    kept, crossed = blocks
    return [half.at[k] for k in range(kept.shape[0]) for half in (kept, crossed)]


def paired(blocks):
    if len(blocks) == 1:
        return [blocks[0]]
    kept, swapped, *chips = blocks
    return [kept.at[0], swapped.at[0]] + [chip.at[core] for chip in chips for core in range(2)]


def fill_bias(peer, swapped, lengths, slot_row, bias):
    rows = slot_row.shape[1]
    own, first = lax.axis_index("dp"), lax.axis_index("ctx") * rows
    slot = jnp.broadcast_to(slot_row[...], (rows, rows))
    along = lax.broadcasted_iota(jnp.int32, (rows, rows), 1)
    down = lax.broadcasted_iota(jnp.int32, (rows, rows), 0)
    key_pos = jnp.sum(jnp.where(slot == down, along, 0), axis=1, keepdims=True)
    slot_down = slot.astype(jnp.float32).T.astype(jnp.int32)
    if swapped:
        mask = jnp.zeros_like(along)
        for index, value in enumerate(MASKS):
            mask = jnp.where(along // peer == index, value, mask)
        wanted = lax.bitwise_xor(mask, own) * peer + along % peer
    else:
        wanted = along
    query_pos = jnp.sum(jnp.where(slot_down == wanted, down, 0), axis=0, keepdims=True)

    def later(k, carry):
        end, start = carry
        end = end + lengths[0, k]
        return end, jnp.where(query_pos + first >= end, end, start)

    _, doc_start = lax.fori_loop(
        0, lengths.shape[1], later, (jnp.int32(0), jnp.zeros((1, rows), jnp.int32))
    )
    seen = (key_pos <= query_pos) & (key_pos + first >= doc_start)
    bias[:rows, :] = jnp.where(seen, 0.0, HIDDEN)
    joined = jnp.where(first < lengths[0, 0], 0.0, HIDDEN).astype(jnp.float32)
    bias[rows:, :] = jnp.full((bias.shape[0] - rows, rows), joined)


def pack_kernel(spots, keys, values, queries, out_grad, lengths, slot_row, *refs):
    kept, crossed, bias, kv, kv_buf, block_buf, query_buf, grad_buf, length_buf, slot_buf, sems = refs
    own = lax.axis_index("dp")
    wide, width = queries.shape[1], keys.shape[2]
    peers, planes, peer = len(spots), len(spots[0]), kv.shape[1]
    come = [
        pltpu.make_async_copy(keys, kv_buf.at[:, :, :width], sems.at[0]),
        pltpu.make_async_copy(values, kv_buf.at[:, :, width:], sems.at[1]),
        pltpu.make_async_copy(queries, query_buf, sems.at[2]),
        pltpu.make_async_copy(out_grad, grad_buf, sems.at[3]),
        pltpu.make_async_copy(lengths, length_buf, sems.at[4]),
        pltpu.make_async_copy(slot_row, slot_buf, sems.at[5]),
    ]
    for copy in come:
        copy.start()
    come[0].wait()
    come[1].wait()
    for d in range(peers):
        block = kv_buf[d]
        for j in range(planes):
            block_buf[spots[d][j]] = block
    leave = pltpu.make_async_copy(block_buf, kv, sems.at[6])
    leave.start()
    come[4].wait()
    come[5].wait()
    fill_bias(peer, True, length_buf, slot_buf, bias)
    for k, buf in enumerate((query_buf, grad_buf)):
        come[2 + k].wait()
        for index, piece in enumerate(parted((kept, crossed))):
            start = pl.multiple_of(lax.bitwise_xor(own, MASKS[index]) * peer, peer)
            piece[:, k * wide : (k + 1) * wide] = buf[pl.ds(start, peer), :]
    leave.wait()


def pair_kernel(kept, swapped, *out):
    for k, block in enumerate(out):
        block[0] = kept[k + 1]
        block[1] = swapped[k + 1]


def core_kernel(heads, taken, spots, bias, kv, *refs):
    planes, plane = len(spots[0][0]), lax.axis_index("ctx")
    if planes > 4:
        core(heads, taken, spots, None, bias, kv, *refs)
        return
    for k in range(planes):
        pl.when(plane == k)(functools.partial(core, heads, taken, spots, k, bias, kv, *refs))


def core(heads, taken, spots, plane, bias, kv, *refs):
    pieces = paired(refs[:taken])
    *returned, kv_grad, key_all, value_all, query_flat, grad_flat, probs_all, score_all = refs[
        taken:-2
    ]
    grad_buf, sem = refs[-2:]
    returned = parted(returned)
    spots_in, spots_out = spots
    peers, planes = len(spots_in), len(spots_in[0])
    _, peer, both = kv.shape
    width = both // 2
    rows = peers * peer
    wide = heads * width
    scale = width**-0.5
    seen, before = bias[:rows, :], bias[rows : rows + 1, :]
    added = []
    for j in range(planes if plane is None else plane + 1):
        if plane is None:
            other = jnp.where(lax.axis_index("ctx") > j, before, HIDDEN)
            added.append(jnp.where(lax.axis_index("ctx") == j, seen, other))
        else:
            added.append(seen if j == plane else jnp.broadcast_to(before, (rows, rows)))
        for d in range(peers):
            at = j * rows + d * peer
            key_all[at : at + peer, :] = kv[spots_in[d][j], :, :width]
            value_all[at : at + peer, :] = kv[spots_in[d][j], :, width:]
    count = len(added) * rows
    added = jnp.concatenate(added, axis=0)
    size = pieces[0].shape[0]
    for index, piece in enumerate(pieces):
        for h in range(heads):
            at = h * rows + index * size
            query_flat[at : at + size, :] = piece[:, h * width : (h + 1) * width]
            grad_flat[at : at + size, :] = piece[:, wide + h * width : wide + (h + 1) * width]
    at_once = 2 if heads % 2 == 0 else 1
    added = jnp.concatenate([added] * at_once, axis=1)
    for h in range(0, heads, at_once):
        own = slice(h * rows, (h + at_once) * rows)
        score = contract(key_all[:count], query_flat[own, :]) * (scale * math.log2(math.e)) + added
        weight = jnp.exp2(score - jnp.max(score, axis=0, keepdims=True))
        probs = weight * (1.0 / jnp.sum(weight, axis=0, keepdims=True))
        prob_grad = contract(value_all[:count], grad_flat[own, :])
        delta = jnp.sum(probs * prob_grad, axis=0, keepdims=True)
        probs_all[:count, own] = probs.astype(jnp.bfloat16)
        score_all[:count, own] = (probs * (prob_grad - delta)).astype(jnp.bfloat16)
    leave = []
    for k, (left, right, factor) in enumerate(
        ((probs_all, grad_flat, None), (score_all, query_flat, scale))
    ):
        half = slice((1 - k) * width, (2 - k) * width)
        total = multiply(left[:count], right[...])
        total = (total if factor is None else total * factor).astype(jnp.bfloat16)
        for j in range(planes):
            for d in range(peers):
                at = j * rows + d * peer
                part = total[at : at + peer] if at < count else jnp.zeros((peer, width), jnp.bfloat16)
                grad_buf[spots_out[d][j], :, half] = part
        leave.append(
            pltpu.make_async_copy(grad_buf.at[:, :, half], kv_grad.at[:, :, half], sem.at[k])
        )
        leave[-1].start()
    attended = multiply(value_all[:count].T, probs_all[:count]).astype(jnp.bfloat16)
    query_grad = (multiply(key_all[:count].T, score_all[:count]) * scale).astype(jnp.bfloat16)
    for k, source in enumerate((attended, query_grad)):
        for h in range(heads):
            turned = source[:, h * rows : (h + 1) * rows].T
            at = (k * heads + h) * width
            for index, piece in enumerate(returned):
                from_row = MASKS.index(MASKS_BACK[index]) * size if len(returned) > 1 else 0
                piece[:, at : at + width] = turned[from_row : from_row + size]
    for copy in leave:
        copy.wait()


def last_kernel(spots, kv, *refs):
    *blocks, attended, query_grad, key_grad, value_grad, key_buf, value_buf, sems = refs
    pieces = paired(blocks)
    wide, size = attended.shape[1], pieces[0].shape[0]
    own = lax.axis_index("dp") if len(pieces) > 1 else None
    copies = []
    for index, piece in enumerate(pieces):
        start = pl.multiple_of(lax.bitwise_xor(own, MASKS_BACK[index]) * size, size) if own is not None else 0
        for k, target in enumerate((attended, query_grad)):
            copies.append(
                pltpu.make_async_copy(
                    piece.at[:, k * wide : (k + 1) * wide],
                    target.at[pl.ds(start, size), :],
                    sems.at[len(copies)],
                )
            )
            copies[-1].start()
    _, peer, both = kv.shape
    width = both // 2
    for k, (buf, target) in enumerate(((key_buf, key_grad), (value_buf, value_grad))):
        part = slice(k * width, (k + 1) * width)
        for d, spot in enumerate(spots):
            total = kv[spot[0], :, part].astype(jnp.float32)
            for block in spot[1:]:
                total = total + kv[block, :, part].astype(jnp.float32)
            buf[d * peer : (d + 1) * peer, :] = total.astype(jnp.bfloat16)
        copies.append(pltpu.make_async_copy(buf, target, sems.at[len(copies)]))
        copies[-1].start()
    for copy in copies:
        copy.wait()


def spots_of(order, peers, planes):
    at = {index: spot for spot, index in enumerate(order or range(peers * planes))}
    return tuple(tuple(at[d * planes + j] for j in range(planes)) for d in range(peers))


def local(queries, keys, values, out_grad, doc_lengths, source_slot):
    rows, wide = queries.shape
    width = keys.shape[1]
    heads = wide // width
    peers, planes = lax.axis_size("dp"), lax.axis_size("ctx")
    peer = rows // peers
    fine = peer % 16 == 0
    swapped = peers == 8 and fine
    kv_shape = (peers * planes, peer, 2 * width)
    measured = swapped and planes == 4
    order_in, order_out = (ORDER_IN, ORDER_OUT) if measured else (None, None)
    if fine:
        spots_in, spots_out = (spots_of(order, peers, planes) for order in (order_in, order_out))
    else:
        spots_in = spots_out = (tuple(range(planes)),)

    def everywhere(x, order):
        groups = [list(order)] if order else None
        return lax.all_to_all(
            x, ("dp", "ctx"), split_axis=0, concat_axis=0, tiled=True, axis_index_groups=groups
        )

    def by_plane(x):
        x = x.reshape(peers, planes, peer, 2 * width)
        return x.transpose(1, 0, 2, 3).reshape(planes, rows, 2 * width)

    def swap(x, mask):
        return lax.ppermute(x, "dp", [(i, i ^ mask) for i in range(peers)])

    def in_plane(pieces, order, cost):
        if not swapped:
            return [lax.all_to_all(pieces[0], "dp", split_axis=0, concat_axis=0, tiled=True)]
        kept, crossed = pieces
        crossed = swap(crossed, 1)
        chips = pl.pallas_call(
            pair_kernel,
            out_shape=[near((2, peer, 2 * wide))] * (peers // 2 - 1),
            in_specs=[VMEM] * 2,
            out_specs=[VMEM] * (peers // 2 - 1),
            compiler_params=params(4),
            cost_estimate=cost,
            name="pair",
        )(kept, crossed)
        return [kept, crossed] + [swap(chip, 2 * mask) for chip, mask in zip(chips, order[1:])]

    slot_row = source_slot.reshape(1, rows)
    if swapped:
        sent = [near((peers // 2, peer, 2 * wide))] * 2
        *pieces, bias, kv = pl.pallas_call(
            functools.partial(pack_kernel, spots_in),
            out_shape=sent + [pltpu.VMEM((rows + 8, rows), jnp.float32), low(kv_shape)],
            in_specs=[HBM] * 6,
            out_specs=[VMEM] * 3 + [HBM],
            scratch_shapes=[
                pltpu.VMEM((peers, peer, 2 * width), jnp.bfloat16),
                pltpu.VMEM(kv_shape, jnp.bfloat16),
                pltpu.VMEM((rows, wide), jnp.bfloat16),
                pltpu.VMEM((rows, wide), jnp.bfloat16),
                pltpu.SMEM(doc_lengths.shape, jnp.int32),
                pltpu.VMEM(slot_row.shape, jnp.int32),
                pltpu.SemaphoreType.DMA((7,)),
            ],
            compiler_params=params(4),
            name="pack",
        )(
            far(keys.reshape(peers, peer, width)),
            far(values.reshape(peers, peer, width)),
            far(queries),
            far(out_grad),
            far(doc_lengths),
            far(slot_row),
        )
    else:
        sent = [low((rows, 2 * wide))]
        kv = jnp.concatenate([keys, values], axis=1).reshape(peers, 1, peer, 2 * width)
        kv = jnp.broadcast_to(kv, (peers, planes, peer, 2 * width)).reshape(kv_shape)
        pieces = [jnp.concatenate([queries, out_grad], axis=1)]
        bias = pl.pallas_call(
            functools.partial(fill_bias, peer, False),
            out_shape=jax.ShapeDtypeStruct((rows + 8, rows), jnp.float32),
            in_specs=[SMEM, VMEM],
            out_specs=VMEM,
            compiler_params=params(4),
            name="mask",
        )(doc_lengths, slot_row)
    kv = everywhere(kv, order_in)
    pieces = in_plane(pieces, CHIPS, pl.CostEstimate(flops=10**10, bytes_accessed=0, transcendentals=0))
    if not fine:
        kv = by_plane(kv)
    count = rows * planes
    *pieces, kv = pl.pallas_call(
        functools.partial(core_kernel, heads, len(pieces), (spots_in, spots_out)),
        out_shape=sent + [low(kv.shape)],
        in_specs=[VMEM] * (2 + len(pieces)),
        out_specs=[VMEM] * len(sent) + [HBM],
        scratch_shapes=[
            pltpu.VMEM((count, width), jnp.bfloat16),
            pltpu.VMEM((count, width), jnp.bfloat16),
            pltpu.VMEM((rows * heads, width), jnp.bfloat16),
            pltpu.VMEM((rows * heads, width), jnp.bfloat16),
            pltpu.VMEM((count, rows * heads), jnp.bfloat16),
            pltpu.VMEM((count, rows * heads), jnp.bfloat16),
            pltpu.VMEM(kv.shape, jnp.bfloat16),
            pltpu.SemaphoreType.DMA((2,)),
        ],
        compiler_params=params(16 if planes <= 4 else 48),
        name="core",
    )(bias, kv, *pieces)
    if not fine:
        kv = kv.reshape(planes, peers, peer, 2 * width).transpose(1, 0, 2, 3).reshape(kv_shape)
    kv = everywhere(kv, order_out)
    if not fine:
        kv = by_plane(kv)
    pieces = in_plane(pieces, CHIPS_BACK, pl.CostEstimate(flops=10**10, bytes_accessed=0, transcendentals=0))
    count = 8 * 2 if swapped else 2
    return tuple(
        pl.pallas_call(
            functools.partial(last_kernel, spots_out),
            out_shape=[low((rows, wide))] * 2 + [low((rows, width))] * 2,
            in_specs=[VMEM] * (1 + len(pieces)),
            out_specs=[HBM] * 4,
            scratch_shapes=[
                pltpu.VMEM((rows, width), jnp.bfloat16),
                pltpu.VMEM((rows, width), jnp.bfloat16),
                pltpu.SemaphoreType.DMA((count + 2,)),
            ],
            compiler_params=params(8),
            name="last",
        )(kv, *pieces)
    )


def solution(mesh):
    rows = P(("dp", "ctx"), None)
    return jax.shard_map(
        local,
        mesh=mesh,
        in_specs=(rows, rows, rows, rows, P("dp", None), P(("dp", "ctx"))),
        out_specs=(rows, rows, rows, rows),
        check_vma=False,
    )
```
